32 devices in a mesh: section: 8 (over z, x), dp: 4 (over y, core).
Axes of the slice: x: 2, y: 2, z: 4, core: 2. Of those that a mesh axis runs over, the one named last changes fastest.
Arguments:
- clip_pool: bfloat16 [16, 3, 4, 2, 640], P('dp'), may hold values from -6 to 6
- sample_ids: int32 [32], P('dp'), may hold values from 0 to 3
- timesteps: int32 [32], P('dp'), may hold values from 0 to 999
- noise_draw: bfloat16 [32, 3, 4, 2, 640], P('dp'), may hold values from -6 to 6
- keep_lists: int32 [32, 16], P('dp'), may hold values 0 or 1
- enc_weight: bfloat16 [8, 5760, 640], P('section'), may hold values from -0.078125 to 0.078125
- enc_gain: float32 [8, 640], P('section'), may hold values from 0.1 to 1.9
- dec_weight: bfloat16 [8, 1920, 640], P('section'), may hold values from -0.125 to 0.125
- dec_gain: float32 [8, 640], P('section'), may hold values from 0.1 to 1.9
Outputs:
- enc_weight_grad: float32 [8, 5760, 640], P('section', 'dp')
- enc_gain_grad: float32 [8, 640], P('section', 'dp')
- dec_weight_grad: float32 [8, 1920, 640], P('section', 'dp')
- dec_gain_grad: float32 [8, 640], P('section', 'dp')
The draws below stay inside these ranges and needn't reach their ends.
All inputs are finite; a program needn't handle non-finite values. No bound on the sum of `keep_lists` on one device may be relied on, other than what follows from the above.
Results may differ from the reference program's by a relative error of at most 0.025.
Values may be sent and summed in bfloat16 or wider, within the bound.
No kernel may reach another device: no remote copies, remote signals or barrier semaphores. Data moves between devices by JAX's collectives and lax.ppermute only.
A program may use at most 64 MiB of HBM per device.

```python
import math
import jax
import jax.numpy as jnp
from jax import lax

CHANNELS = 640
GROUPS = 32
FRAMES = 3
HEIGHT = 4
WIDTH = 2
MICRO = 8
POOL_DEV = 4
LEVELS = 8
SAMPLES = 32
POOL = 16


def touch_ends(result, rng, least, top_value):
    longest = result.shape.index(max(result.shape))
    spots = []
    for shift in (0, 1):
        where = [jax.random.randint(jax.random.fold_in(rng, axis), (), 0, length) for axis, length in enumerate(result.shape)]
        where[longest] = (where[longest] + shift) % result.shape[longest]
        spots.append(tuple(where))
    return result.at[spots[0]].set(least).at[spots[1]].set(top_value)


def levels(own_key, extent, split, least, largest):
    gain = 1.0
    for dim, blocks in split:
        heights = jax.random.uniform(jax.random.fold_in(jax.random.fold_in(own_key, 6), dim), (blocks,), jnp.float32, least / len(split), largest / len(split))
        gain = gain * jnp.repeat(jnp.exp(heights), extent[dim] // blocks).reshape((-1,) + (1,) * (len(extent) - 1 - dim))
    return gain


def gaussian(key, shape, deviation, most, split=(), kind=jnp.bfloat16):
    loudness = levels(key, shape, split, -0.22, 0.18) if split else 1.0
    drawn = jax.random.normal(key, shape, jnp.float32) * deviation * loudness
    return jnp.minimum(jnp.maximum(drawn, -most), most).astype(kind)


def setup_inputs(seed: int = 0) -> dict:
    key_of = jax.random.split(jax.random.key(seed), 10)
    clip_pool = gaussian(key_of[0], (POOL, FRAMES, HEIGHT, WIDTH, CHANNELS), 1.0, 6.0, ((0, 4),))
    sample_ids = touch_ends(jax.random.randint(key_of[1], (SAMPLES,), 0, POOL_DEV), jax.random.fold_in(key_of[1], 1), 0, POOL_DEV - 1).astype(jnp.int32)
    timesteps = touch_ends(jax.random.randint(key_of[2], (SAMPLES,), 0, 1000), jax.random.fold_in(key_of[2], 1), 0, 999).astype(jnp.int32)
    noise_draw = gaussian(key_of[3], (SAMPLES, FRAMES, HEIGHT, WIDTH, CHANNELS), 1.0, 6.0, ((0, 4),))
    keep_lists = touch_ends((jax.random.randint(key_of[4], (SAMPLES, 2 * LEVELS), 0, 4) < 3).astype(jnp.int32), jax.random.fold_in(key_of[4], 1), 0, 1)
    enc_weight = gaussian(key_of[5], (LEVELS, 9 * CHANNELS, CHANNELS), (9 * CHANNELS) ** -0.5, 0.078125, ((0, 8),))
    enc_gain = jnp.clip(1.0 + 0.18 * jax.random.normal(key_of[6], (LEVELS, CHANNELS), jnp.float32), 0.1, 1.9)
    dec_weight = gaussian(key_of[7], (LEVELS, 3 * CHANNELS, CHANNELS), (3 * CHANNELS) ** -0.5, 0.125, ((0, 8),))
    dec_gain = jnp.clip(1.0 + 0.18 * jax.random.normal(key_of[8], (LEVELS, CHANNELS), jnp.float32), 0.1, 1.9)
    return dict(clip_pool=clip_pool, sample_ids=sample_ids, timesteps=timesteps, noise_draw=noise_draw, keep_lists=keep_lists, enc_weight=enc_weight, enc_gain=enc_gain, dec_weight=dec_weight, dec_gain=dec_gain)


def noise_level(timesteps):
    phase_arg = (timesteps.astype(jnp.float32) / 1000.0 + 0.008) / 1.008
    return jnp.cos(phase_arg * (math.pi / 2.0)) ** 2

def norm_act(values, gain_rows):
    batch_size = values.shape[0]
    channels = values.shape[-1]
    grouped = values.reshape(batch_size, -1, GROUPS, channels // GROUPS)
    center = grouped - lax.optimization_barrier(jnp.mean(grouped, axis=(1, 3), keepdims=True))
    spread = lax.optimization_barrier(jnp.mean(center * center, axis=(1, 3), keepdims=True))
    normed = (center * lax.rsqrt(spread + 1e-05)).reshape(values.shape)
    return jax.nn.silu(normed * gain_rows[:, None, None, None, :])

def spatial_columns(activation):
    grid_height = activation.shape[2]
    grid_width = activation.shape[3]
    padded = jnp.pad(activation, ((0, 0), (0, 0), (1, 1), (1, 1), (0, 0)))
    pieces = [padded[:, :, row_shift:row_shift + grid_height, col_shift:col_shift + grid_width, :] for row_shift in range(3) for col_shift in range(3)]
    return jnp.concatenate(pieces, axis=-1).reshape(-1, 9 * activation.shape[-1])

def spatial_spread(columns, full_shape):
    batch_size, frames, grid_height, grid_width, channels = full_shape
    columns = columns.reshape(batch_size, frames, grid_height, grid_width, 9, channels)
    summed = jnp.zeros((batch_size, frames, grid_height + 2, grid_width + 2, channels), jnp.float32)
    for kernel_tap in range(9):
        row_shift = kernel_tap // 3
        col_shift = kernel_tap % 3
        summed = summed + jnp.pad(columns[:, :, :, :, kernel_tap, :], ((0, 0), (0, 0), (row_shift, 2 - row_shift), (col_shift, 2 - col_shift), (0, 0)))
    return summed[:, :, 1:grid_height + 1, 1:grid_width + 1, :]

def temporal_columns(activation):
    frames = activation.shape[1]
    padded = jnp.pad(activation, ((0, 0), (1, 1), (0, 0), (0, 0), (0, 0)))
    pieces = [padded[:, frame_shift:frame_shift + frames] for frame_shift in range(3)]
    return jnp.concatenate(pieces, axis=-1).reshape(-1, 3 * activation.shape[-1])

def temporal_spread(columns, full_shape):
    batch_size, frames, grid_height, grid_width, channels = full_shape
    columns = columns.reshape(batch_size, frames, grid_height, grid_width, 3, channels)
    summed = jnp.zeros((batch_size, frames + 2, grid_height, grid_width, channels), jnp.float32)
    for kernel_tap in range(3):
        summed = summed + jnp.pad(columns[:, :, :, :, kernel_tap, :], ((0, 0), (kernel_tap, 2 - kernel_tap), (0, 0), (0, 0), (0, 0)))
    return summed[:, 1:frames + 1]

def gate_shape(keep_rate):
    return keep_rate[:, None, None, None, None]

def encoder_forward(stream, weight, gain_rows, keep_rate):
    activation = norm_act(stream.astype(jnp.float32), gain_rows).astype(jnp.bfloat16)
    branch = jnp.dot(spatial_columns(activation), weight, preferred_element_type=jnp.float32)
    return (stream.astype(jnp.float32) + gate_shape(keep_rate) * branch.reshape(stream.shape)).astype(jnp.bfloat16)

def encoder_backward(stream, upstream, weight, gain_rows, keep_rate):
    activation, pullback = jax.vjp(norm_act, stream.astype(jnp.float32), gain_rows)
    columns = spatial_columns(activation.astype(jnp.bfloat16))
    gated = (gate_shape(keep_rate) * upstream.astype(jnp.float32)).astype(jnp.bfloat16).reshape(-1, stream.shape[-1])
    back_cols = lax.dot_general(gated, weight, (((1,), (1,)), ((), ())), preferred_element_type=jnp.float32)
    norm_grad, gain_grad = pullback(spatial_spread(back_cols, stream.shape))
    stream_grad = (upstream.astype(jnp.float32) + norm_grad).astype(jnp.bfloat16)
    return (stream_grad, columns, gated, gain_grad)

def decoder_forward(stream, skip_act, weight, gain_rows, keep_rate):
    merged = stream.astype(jnp.float32) + skip_act.astype(jnp.float32)
    activation = norm_act(merged, gain_rows).astype(jnp.bfloat16)
    branch = jnp.dot(temporal_columns(activation), weight, preferred_element_type=jnp.float32)
    return (stream.astype(jnp.float32) + gate_shape(keep_rate) * branch.reshape(stream.shape)).astype(jnp.bfloat16)

def decoder_backward(stream, skip_act, upstream, weight, gain_rows, keep_rate):
    merged = stream.astype(jnp.float32) + skip_act.astype(jnp.float32)
    activation, pullback = jax.vjp(norm_act, merged, gain_rows)
    columns = temporal_columns(activation.astype(jnp.bfloat16))
    gated = (gate_shape(keep_rate) * upstream.astype(jnp.float32)).astype(jnp.bfloat16).reshape(-1, stream.shape[-1])
    back_cols = lax.dot_general(gated, weight, (((1,), (1,)), ((), ())), preferred_element_type=jnp.float32)
    merged_grad, gain_grad = pullback(temporal_spread(back_cols, stream.shape))
    stream_grad = (upstream.astype(jnp.float32) + merged_grad).astype(jnp.bfloat16)
    return (stream_grad, merged_grad.astype(jnp.bfloat16), columns, gated, gain_grad)

def group_total(terms):
    grouped = terms.reshape((SAMPLES // MICRO, MICRO) + terms.shape[1:]).sum(axis=1)
    rounded = lax.optimization_barrier(grouped.astype(jnp.bfloat16))
    return lax.optimization_barrier(jnp.sum(rounded.astype(jnp.float32), axis=0))

def weight_total(columns, gated):
    group_count = SAMPLES // MICRO
    left_rows = columns.reshape(group_count, -1, columns.shape[-1]).astype(jnp.float32)
    right_rows = gated.reshape(group_count, -1, gated.shape[-1]).astype(jnp.float32)
    per_group = jnp.einsum('gtk,gtc->gkc', left_rows, right_rows, precision=lax.Precision.HIGHEST)
    rounded = lax.optimization_barrier(per_group.astype(jnp.bfloat16))
    return lax.optimization_barrier(jnp.sum(rounded.astype(jnp.float32), axis=0))

def reference(clip_pool, sample_ids, timesteps, noise_draw, keep_lists, enc_weight, enc_gain, dec_weight, dec_gain):
    owners = jnp.arange(SAMPLES, dtype=jnp.int32) // MICRO * POOL_DEV + sample_ids.astype(jnp.int32)
    clean = jnp.take(clip_pool, owners, axis=0).astype(jnp.float32)
    level_noise = noise_level(timesteps)[:, None, None, None, None]
    stream = (jnp.sqrt(level_noise) * clean + jnp.sqrt(1.0 - level_noise) * noise_draw.astype(jnp.float32)).astype(jnp.bfloat16)
    keep_rates = keep_lists.astype(jnp.float32)
    enc_inputs = []
    skip_acts = []
    for level_index in range(LEVELS):
        gain_rows = jnp.broadcast_to(enc_gain[level_index], (SAMPLES, CHANNELS))
        enc_inputs.append(stream)
        stream = encoder_forward(stream, enc_weight[level_index], gain_rows, keep_rates[:, level_index])
        skip_acts.append(stream)
    dec_inputs = []
    for level_index in range(LEVELS):
        gain_rows = jnp.broadcast_to(dec_gain[level_index], (SAMPLES, CHANNELS))
        dec_inputs.append(stream)
        stream = decoder_forward(stream, skip_acts[LEVELS - 1 - level_index], dec_weight[level_index], gain_rows, keep_rates[:, LEVELS + level_index])
    scale = 1.0 / math.sqrt(SAMPLES * FRAMES * HEIGHT * WIDTH)
    upstream = ((stream.astype(jnp.float32) - noise_draw.astype(jnp.float32)) * scale).astype(jnp.bfloat16)
    dec_weight_terms = [None] * LEVELS
    dec_gain_terms = [None] * LEVELS
    skip_grads = [None] * LEVELS
    for level_index in reversed(range(LEVELS)):
        gain_rows = jnp.broadcast_to(dec_gain[level_index], (SAMPLES, CHANNELS))
        stream_grad, skip_grad, columns, gated, gain_grad = decoder_backward(dec_inputs[level_index], skip_acts[LEVELS - 1 - level_index], upstream, dec_weight[level_index], gain_rows, keep_rates[:, LEVELS + level_index])
        dec_weight_terms[level_index] = weight_total(columns, gated)
        dec_gain_terms[level_index] = group_total(gain_grad)
        skip_grads[LEVELS - 1 - level_index] = skip_grad
        upstream = stream_grad
    enc_weight_terms = [None] * LEVELS
    enc_gain_terms = [None] * LEVELS
    for level_index in reversed(range(LEVELS)):
        gain_rows = jnp.broadcast_to(enc_gain[level_index], (SAMPLES, CHANNELS))
        summed_grad = (upstream.astype(jnp.float32) + skip_grads[level_index].astype(jnp.float32)).astype(jnp.bfloat16)
        stream_grad, columns, gated, gain_grad = encoder_backward(enc_inputs[level_index], summed_grad, enc_weight[level_index], gain_rows, keep_rates[:, level_index])
        enc_weight_terms[level_index] = weight_total(columns, gated)
        enc_gain_terms[level_index] = group_total(gain_grad)
        upstream = stream_grad
    return (jnp.stack(enc_weight_terms), jnp.stack(enc_gain_terms), jnp.stack(dec_weight_terms), jnp.stack(dec_gain_terms))
```

```python
import functools
import math

import jax
import jax.numpy as jnp
import numpy as np
from jax import lax
from jax.experimental import pallas as pl
from jax.experimental.pallas import tpu as pltpu
from jax.sharding import PartitionSpec as P

GROUPS = 32
ENC_TAPS = 9
DEC_TAPS = 3
KERNELS_OF_A_CHAIN = 32
BF16 = jnp.bfloat16
F32 = jnp.float32
VMEM_LIMIT = 32 * 1024 * 1024


def noise_level(timesteps):
    phase_arg = (timesteps.astype(F32) / 1000.0 + 0.008) / 1.008
    return jnp.cos(phase_arg * (math.pi / 2.0)) ** 2


def group_means(sums, spread_matrix, count, splits):
    rest = sums
    pieces = []
    for _ in range(splits - 1):
        piece = rest.astype(BF16).astype(F32)
        pieces.append(piece)
        rest = rest - piece
    pieces.append(rest)
    number = sums.shape[0]
    parts = jnp.concatenate(pieces, axis=0).astype(BF16)
    spread = jnp.dot(parts, spread_matrix, preferred_element_type=F32)
    total = spread[:number]
    for place in range(1, splits):
        total = total + spread[place * number : (place + 1) * number]
    folded = total.reshape(number // 8, 8, sums.shape[1])
    return jnp.sum(folded, axis=1, keepdims=True) * (1.0 / count)


def eight_rows(values):
    return jnp.sum(values.reshape(-1, 8, values.shape[-1]), axis=0)


def sigmoid(z):
    return 0.5 * jnp.tanh(0.5 * z) + 0.5


def spatial_shift(frames, row_offset, col_offset, height, width):
    step = row_offset * width + col_offset
    length = height * width
    moved = pltpu.roll(frames, (-step) % length, axis=1) if step % length else frames
    if row_offset == 0 and col_offset == 0:
        return moved
    place = lax.broadcasted_iota(jnp.int32, (1, length, 1), 1)
    row = place // width + row_offset
    col = place % width + col_offset
    inside = (row >= 0) & (row < height) & (col >= 0) & (col < width)
    return jnp.where(inside, moved, 0.0)


def spatial_columns_into(cols_ref, values_ref, sizes, sign):
    each = sizes.height * sizes.width
    pair = 2 * each
    channels = sizes.channels

    def one_pair(index, carry):
        place = pl.ds(pl.multiple_of(index * pair, pair), pair)
        frames = values_ref[place].reshape(2, each, channels)
        for tap in range(ENC_TAPS):
            moved = spatial_shift(
                frames, sign * (tap // 3 - 1), sign * (tap % 3 - 1), sizes.height, sizes.width
            )
            cols_ref[tap // 3, place, (tap % 3) * channels : (tap % 3 + 1) * channels] = (
                moved.reshape(pair, channels).astype(BF16)
            )
        return carry

    lax.fori_loop(0, sizes.rows // pair, one_pair, 0)


def temporal_pieces(values, frames, sign):
    samples, length, channels = values.shape
    each = length // frames
    blank = jnp.zeros((samples, each, channels), F32)
    before = jnp.concatenate([blank, values[:, : length - each]], axis=1)
    after = jnp.concatenate([values[:, each:], blank], axis=1)
    ordered = (before, values, after) if sign > 0 else (after, values, before)
    return [piece.reshape(samples * length, channels).astype(BF16) for piece in ordered]


def dot_nt(left, right):
    return lax.dot_general(left, right, (((1,), (1,)), ((), ())), preferred_element_type=F32)


class Sizes:
    def __init__(self, noise_draw, sections):
        self.micro, self.frames, self.height, self.width, self.channels = noise_draw.shape
        self.length = self.frames * self.height * self.width
        self.per_step = max(1, self.micro * sections // KERNELS_OF_A_CHAIN)
        self.steps = self.micro // self.per_step
        self.rows = self.per_step * self.length
        self.count = self.length * (self.channels // GROUPS)
        self.total = self.micro * self.length

    def sample(self, index):
        return slice(index * self.length, (index + 1) * self.length)


def norm_forward(sizes, step, values_ref, gain, spread_matrix, xhat_ref, rstd_ref):
    samples = range(sizes.per_step)
    sums = jnp.concatenate([eight_rows(values_ref[sizes.sample(s)]) for s in samples], axis=0)
    mean = group_means(sums, spread_matrix, sizes.count, 3)
    squares = []
    for s in samples:
        center = values_ref[sizes.sample(s)] - mean[s]
        values_ref[sizes.sample(s)] = center
        squares.append(eight_rows(center * center))
    spread = group_means(jnp.concatenate(squares, axis=0), spread_matrix, sizes.count, 3)
    rstd = lax.rsqrt(spread + 1e-05)
    for s in samples:
        first = step * sizes.rows + s * sizes.length
        normed = values_ref[sizes.sample(s)] * rstd[s]
        xhat_ref[first : first + sizes.length] = normed
        rstd_ref[step * sizes.per_step + s] = rstd[s]
        z = normed * gain
        values_ref[sizes.sample(s)] = z * sigmoid(z)


def residual(sizes, step, base_ref, keep_ref, branch_ref):
    out = []
    for s in range(sizes.per_step):
        index = step * sizes.per_step + s
        keep = keep_ref[index : index + 1]
        out.append(base_ref[sizes.sample(s)] + keep * branch_ref[sizes.sample(s)])
    return jnp.concatenate(out, axis=0)


def enc_forward_kernel(sizes, level, step, x_ref, w_ref, gain_ref, keep_ref, spread_ref, *refs):
    y_ref, xhat_ref, rstd_ref, act_ref, cols_ref, base_ref, values_ref, half_ref, sem = refs[-9:]

    @pl.when(lax.axis_index("section") == level)
    def _():
        x = x_ref[...].astype(F32)
        base_ref[...] = x
        values_ref[...] = x
        norm_forward(
            sizes, step, values_ref, gain_ref[...], spread_ref[...], xhat_ref, rstd_ref
        )
        half_ref[...] = values_ref[...].astype(BF16)
        part = pl.ds(step * sizes.rows, sizes.rows)
        store = pltpu.make_async_copy(half_ref, act_ref.at[part], sem)
        store.start()
        spatial_columns_into(cols_ref, values_ref, sizes, 1)

        def add_third(third, carry):
            part = jnp.dot(cols_ref[third], w_ref[third], preferred_element_type=F32)
            values_ref[...] = jnp.where(third == 0, part, values_ref[...] + part)
            return carry

        lax.fori_loop(0, 3, add_third, 0)
        y_ref[...] = residual(sizes, step, base_ref, keep_ref, values_ref).astype(BF16)
        store.wait()


def dec_forward_kernel(
    sizes, level, step, first, scale, x_ref, skip_ref, w_ref, gain_ref, keep_ref, spread_ref, *refs
):
    y_ref, xhat_ref, rstd_ref, act_ref, base_ref, values_ref, half_ref, sem = refs[-8:]

    @pl.when(lax.axis_index("section") == level)
    def _():
        x = x_ref[...].astype(F32)
        base_ref[...] = x
        values_ref[...] = x + (x if first else skip_ref[...].astype(F32))
        norm_forward(
            sizes, step, values_ref, gain_ref[...], spread_ref[...], xhat_ref, rstd_ref
        )
        half_ref[...] = values_ref[...].astype(BF16)
        part = pl.ds(step * sizes.rows, sizes.rows)
        store = pltpu.make_async_copy(half_ref, act_ref.at[part], sem)
        store.start()
        act = values_ref[...].reshape(sizes.per_step, sizes.length, sizes.channels)
        columns = jnp.concatenate(temporal_pieces(act, sizes.frames, 1), axis=1)
        values_ref[...] = jnp.dot(columns, w_ref[...], preferred_element_type=F32)
        out = residual(sizes, step, base_ref, keep_ref, values_ref).astype(BF16)
        if scale is not None:
            noise_ref = refs[0]
            out = ((out.astype(F32) - noise_ref[part].astype(F32)) * scale).astype(BF16)
        y_ref[...] = out
        store.wait()


def norm_back(sizes, step, cot_ref, gain, spread_matrix, xhat_ref, rstd_ref):
    samples = range(sizes.per_step)
    sums, products = [], []
    gain_rows = 0.0
    for s in samples:
        first = step * sizes.rows + s * sizes.length
        normed = xhat_ref[first : first + sizes.length]
        z = normed * gain
        sig = sigmoid(z)
        dz = cot_ref[sizes.sample(s)] * (sig * (1.0 + z * (1.0 - sig)))
        gain_rows = gain_rows + eight_rows(dz * normed)
        dn = dz * gain
        cot_ref[sizes.sample(s)] = dn
        sums.append(eight_rows(dn))
        products.append(eight_rows(dn * normed))
    means = group_means(jnp.concatenate(sums + products, axis=0), spread_matrix, sizes.count, 2)
    for s in samples:
        first = step * sizes.rows + s * sizes.length
        normed = xhat_ref[first : first + sizes.length]
        rstd = rstd_ref[step * sizes.per_step + s]
        cot_ref[sizes.sample(s)] = rstd * (
            cot_ref[sizes.sample(s)] - means[s] - normed * means[sizes.per_step + s]
        )
    return gain_rows


def add_gain(sizes, step, gain_acc_ref, gain_rows, cot_ref, half_ref, sem):
    total = gain_rows if step == 0 else gain_acc_ref[...] + gain_rows
    gain_acc_ref[...] = total
    if step == sizes.steps - 1:
        row = jnp.sum(total, axis=0, keepdims=True)
        tail = jnp.concatenate([row, jnp.zeros((15, sizes.channels), F32)], axis=0)
        half_ref[:16] = tail.astype(BF16)
        copy = pltpu.make_async_copy(
            half_ref.at[pl.ds(0, 16)], cot_ref.at[pl.ds(sizes.total, 16)], sem
        )
        copy.start()
        copy.wait()


def gate(sizes, step, keep_ref, values):
    out = []
    for s in range(sizes.per_step):
        index = step * sizes.per_step + s
        out.append(keep_ref[index : index + 1] * values[sizes.sample(s)])
    return jnp.concatenate(out, axis=0)


def enc_backward_kernel(
    sizes, level, step, last, x_ref, skip_ref, w_ref, gain_ref, keep_ref, spread_ref, xhat_ref, rstd_ref, *refs
):
    y_ref, gain_acc_ref, cot_ref, cols_ref, base_ref, values_ref, half_ref, sem = refs[-8:]

    @pl.when(lax.axis_index("section") == level)
    def _():
        t = x_ref[...]
        if not last:
            t = (t.astype(F32) + skip_ref[...].astype(F32)).astype(BF16)
        t = t.astype(F32)
        base_ref[...] = t
        gated = gate(sizes, step, keep_ref, t)
        values_ref[...] = gated
        half_ref[...] = gated.astype(BF16)
        part = pl.ds(step * sizes.rows, sizes.rows)
        store = pltpu.make_async_copy(half_ref, cot_ref.at[part], sem)
        store.start()
        spatial_columns_into(cols_ref, values_ref, sizes, -1)

        def add_third(third, carry):
            part = jnp.zeros((sizes.rows, sizes.channels), F32)
            for tap in range(3):
                where = slice(tap * sizes.channels, (tap + 1) * sizes.channels)
                part = part + dot_nt(cols_ref[third, :, where], w_ref[third, where, :])
            values_ref[...] = jnp.where(third == 0, part, values_ref[...] + part)
            return carry

        lax.fori_loop(0, 3, add_third, 0)
        gain_rows = norm_back(
            sizes, step, values_ref, gain_ref[...], spread_ref[...], xhat_ref, rstd_ref
        )
        y_ref[...] = (base_ref[...] + values_ref[...]).astype(BF16)
        store.wait()
        add_gain(sizes, step, gain_acc_ref, gain_rows, cot_ref, half_ref, sem)


def dec_backward_kernel(
    sizes, level, step, first, x_ref, w_ref, gain_ref, keep_ref, spread_ref, xhat_ref, rstd_ref, *refs
):
    y_ref = refs[-8 if not first else -7]
    skip_cot_ref = refs[-7]
    gain_acc_ref, cot_ref, base_ref, values_ref, half_ref, sem = refs[-6:]

    @pl.when(lax.axis_index("section") == level)
    def _():
        g = x_ref[...].astype(F32)
        base_ref[...] = g
        gated = gate(sizes, step, keep_ref, g)
        half_ref[...] = gated.astype(BF16)
        part = pl.ds(step * sizes.rows, sizes.rows)
        store = pltpu.make_async_copy(half_ref, cot_ref.at[part], sem)
        store.start()
        pieces = temporal_pieces(
            gated.reshape(sizes.per_step, sizes.length, sizes.channels), sizes.frames, -1
        )
        back = jnp.zeros((sizes.rows, sizes.channels), F32)
        for tap in range(DEC_TAPS):
            where = slice(tap * sizes.channels, (tap + 1) * sizes.channels)
            back = back + dot_nt(pieces[tap], w_ref[where, :])
        values_ref[...] = back
        gain_rows = norm_back(
            sizes, step, values_ref, gain_ref[...], spread_ref[...], xhat_ref, rstd_ref
        )
        grad = values_ref[...]
        out = (base_ref[...] + grad).astype(BF16)
        skip_cot = grad.astype(BF16)
        if first:
            out = (out.astype(F32) + skip_cot.astype(F32)).astype(BF16)
        else:
            skip_cot_ref[...] = skip_cot
        y_ref[...] = out
        store.wait()
        add_gain(sizes, step, gain_acc_ref, gain_rows, cot_ref, half_ref, sem)


def tap_span(rows_out, channels, taps, parts):
    span = 0
    for index in range(parts):
        start = index * rows_out
        span = max(span, -(-(start % channels + rows_out) // channels))
    return min(span, taps)


def weight_kernel(sizes, taps, span, rows_out, act_ref, cot_ref, out_ref, gain_out_ref, wide_ref):
    me = lax.axis_index("dp")
    groups = act_ref.shape[0]
    valid = sizes.micro * sizes.length
    rows = groups * valid
    base = jnp.minimum(me * rows_out // sizes.channels, taps - span)
    act = act_ref[...].reshape(rows, sizes.channels).astype(F32)
    cot = cot_ref[:, :valid, :].reshape(rows, sizes.channels)
    each = sizes.height * sizes.width
    gain_out_ref[...] = jnp.sum(cot_ref[:, valid : valid + 16, :].astype(F32), axis=0)[:8]
    for tap in range(taps):

        @pl.when((tap >= base) & (tap < base + span))
        def _(tap=tap):
            if taps == ENC_TAPS:
                frames = act.reshape(rows // each, each, sizes.channels)
                moved = spatial_shift(frames, tap // 3 - 1, tap % 3 - 1, sizes.height, sizes.width)
                moved = moved.reshape(rows, sizes.channels).astype(BF16)
            else:
                values = act.reshape(rows // sizes.length, sizes.length, sizes.channels)
                moved = temporal_pieces(values, sizes.frames, 1)[tap]
            place = pl.multiple_of((tap - base) * sizes.channels, sizes.channels)
            wide_ref[pl.ds(place, sizes.channels)] = lax.dot_general(
                moved, cot, (((0,), (0,)), ((), ())), preferred_element_type=F32
            )

    offset = pl.multiple_of(me * rows_out - base * sizes.channels, 16)
    out_ref[...] = wide_ref[pl.ds(offset, rows_out)]


def load_kernel(enc_ref, dec_ref, spread_ref, enc_out, dec_out, spread_out, sems):
    copies = [
        pltpu.make_async_copy(enc_ref, enc_out, sems.at[0]),
        pltpu.make_async_copy(dec_ref, dec_out, sems.at[1]),
        pltpu.make_async_copy(spread_ref, spread_out, sems.at[2]),
    ]
    for copy in copies:
        copy.start()
    for copy in copies:
        copy.wait()


VM = pl.BlockSpec(memory_space=pltpu.VMEM)
ANY = pl.BlockSpec(memory_space=pl.ANY)


def params():
    return pltpu.CompilerParams(vmem_limit_bytes=VMEM_LIMIT)


def in_vmem(value):
    return pltpu.with_memory_space_constraint(value, pltpu.VMEM)


def staged_call(kernel, inputs, plain_outs, kept, far, state, scratch, flops):
    number = len(inputs)
    inputs = [in_vmem(value) for value in inputs]
    in_specs = [VM] * number
    aliases = {}
    if state is not None:
        for place in range(len(state)):
            aliases[number + place] = len(plain_outs) + place
        inputs = inputs + [in_vmem(value) for value in state[: len(kept)]] + list(state[len(kept) :])
        in_specs = in_specs + [VM] * len(kept) + [ANY] * len(far)
    outs = pl.pallas_call(
        kernel,
        in_specs=in_specs,
        out_specs=[VM] * (len(plain_outs) + len(kept)) + [ANY] * len(far),
        out_shape=[pltpu.VMEM(s, d) for s, d in list(plain_outs) + list(kept)]
        + [jax.ShapeDtypeStruct(s, d) for s, d in far],
        scratch_shapes=scratch,
        input_output_aliases=aliases,
        compiler_params=params(),
        cost_estimate=pl.CostEstimate(flops=flops, bytes_accessed=0, transcendentals=0),
    )(*inputs)
    return outs[: len(plain_outs)], outs[len(plain_outs) :]


def body(
    clip_pool,
    sample_ids,
    timesteps,
    noise_draw,
    keep_lists,
    enc_weight,
    enc_gain,
    dec_weight,
    dec_gain,
):
    sections = lax.axis_size("section")
    parts = lax.axis_size("dp")
    own_level = lax.axis_index("section")
    sizes = Sizes(noise_draw, sections)
    channels, rows, steps = sizes.channels, sizes.rows, sizes.steps
    total_rows = sizes.total
    scale = 1.0 / math.sqrt(sizes.micro * parts * sizes.length)

    channel = np.arange(channels) // (channels // GROUPS)
    spread_matrix = jnp.asarray(channel[:, None] == channel[None, :], BF16)
    enc_taps = enc_weight.reshape(3, 3 * channels, channels)
    dec_taps = dec_weight.reshape(DEC_TAPS * channels, channels)
    enc_taps, dec_taps, spread_matrix = pl.pallas_call(
        load_kernel,
        in_specs=[ANY] * 3,
        out_specs=[VM] * 3,
        out_shape=[
            pltpu.VMEM(enc_taps.shape, BF16),
            pltpu.VMEM(dec_taps.shape, BF16),
            pltpu.VMEM(spread_matrix.shape, BF16),
        ],
        scratch_shapes=[pltpu.SemaphoreType.DMA((3,))],
        compiler_params=params(),
    )(enc_taps, dec_taps, spread_matrix)

    keep_rates = keep_lists.astype(F32)
    own_keep = [
        jnp.broadcast_to(
            lax.dynamic_slice_in_dim(keep_rates, own_level + shift, 1, 1), (sizes.micro, channels)
        )
        for shift in (0, sections)
    ]
    clean = jnp.take(clip_pool, sample_ids, axis=0).astype(F32)
    level_noise = noise_level(timesteps)[:, None, None, None, None]
    start = (
        jnp.sqrt(level_noise) * clean + jnp.sqrt(1.0 - level_noise) * noise_draw.astype(F32)
    ).astype(BF16)
    start = start.reshape(steps, rows, channels)
    noise_rows = noise_draw.reshape(total_rows, channels)

    row_shape = ((rows, channels), BF16)
    forward_state = (
        [((total_rows, channels), F32), ((sizes.micro, 1, channels), F32)],
        [((total_rows, channels), BF16)],
    )
    back_state = ([((8, channels), F32)], [((total_rows + 16, channels), BF16)])
    work = [
        pltpu.VMEM((rows, channels), F32),
        pltpu.VMEM((rows, channels), F32),
        pltpu.VMEM((rows, channels), BF16),
        pltpu.SemaphoreType.DMA,
    ]
    cols = [pltpu.VMEM((3, rows, 3 * channels), BF16)] + work
    enc_flops = 2 * rows * ENC_TAPS * channels * channels
    dec_flops = 2 * rows * DEC_TAPS * channels * channels

    def send(value, source, target):
        return lax.ppermute(value, "section", [(source, target)])

    last = sections - 1
    current = [start[step] for step in range(steps)]
    skips = [None] * sections
    enc_state = None
    for level in range(sections):
        sent = []
        skip = []
        for step in range(steps):
            (y,), enc_state = staged_call(
                functools.partial(enc_forward_kernel, sizes, level, step),
                [current[step], enc_taps, enc_gain, own_keep[0], spread_matrix],
                [row_shape],
                *forward_state,
                enc_state,
                cols,
                enc_flops,
            )
            sent.append(send(y, level, (level + 1) % sections))
            if level < last:
                skip.append(send(y, level, last - level))
        current = sent
        skips[level] = skip
    enc_xhat, enc_rstd, enc_act = enc_state
    enc_act_all = lax.all_gather(enc_act, "dp")

    dec_state = None
    for level in range(sections):
        sent = []
        for step in range(steps):
            first = level == 0
            skip = current[step] if first else skips[last - level][step]
            final = level == last
            extra = [noise_rows] if final else []
            kernel = functools.partial(
                dec_forward_kernel, sizes, level, step, first, scale if final else None
            )
            inputs = [current[step], skip, dec_taps, dec_gain, own_keep[1], spread_matrix] + extra
            (y,), dec_state = staged_call(
                kernel, inputs, [row_shape], *forward_state, dec_state, work, dec_flops
            )
            sent.append(y if final else send(y, level, level + 1))
        current = sent
    dec_xhat, dec_rstd, dec_act = dec_state
    dec_act_all = lax.all_gather(dec_act, "dp")

    skip_cots = [None] * sections
    state = None
    for level in reversed(range(sections)):
        sent = []
        cots = []
        first = level == 0
        for step in range(steps):
            outs, state = staged_call(
                functools.partial(dec_backward_kernel, sizes, level, step, first),
                [current[step], dec_taps, dec_gain, own_keep[1], spread_matrix, dec_xhat, dec_rstd],
                [row_shape] if first else [row_shape, row_shape],
                *back_state,
                state,
                work,
                dec_flops,
            )
            sent.append(send(outs[0], level, last if first else level - 1))
            if not first:
                cots.append(send(outs[1], level, last - level))
        current = sent
        skip_cots[last - level] = cots
    dec_cot_all = lax.all_gather(state[1], "dp")

    def weight_grad(act_all, cot_all, taps):
        rows_out = taps * channels // parts
        span = tap_span(rows_out, channels, taps, parts)
        grad, gain = pl.pallas_call(
            functools.partial(weight_kernel, sizes, taps, span, rows_out),
            in_specs=[VM, VM],
            out_specs=[VM, VM],
            out_shape=[
                jax.ShapeDtypeStruct((rows_out, channels), F32),
                jax.ShapeDtypeStruct((8, channels), F32),
            ],
            scratch_shapes=[pltpu.VMEM((span * channels, channels), F32)],
            compiler_params=params(),
            cost_estimate=pl.CostEstimate(
                flops=2 * span * channels * channels * parts * total_rows,
                bytes_accessed=rows_out * channels * 4,
                transcendentals=0,
            ),
        )(act_all, cot_all)
        width = channels // parts
        own = lax.axis_index("dp") * width
        return grad, lax.dynamic_slice(gain, (0, own), (1, width))

    dec_weight_out, dec_gain_out = weight_grad(dec_act_all, dec_cot_all, DEC_TAPS)

    state = None
    for level in reversed(range(sections)):
        sent = []
        final = level == last
        for step in range(steps):
            skip = current[step] if final else skip_cots[level][step]
            (y,), state = staged_call(
                functools.partial(enc_backward_kernel, sizes, level, step, final),
                [current[step], skip, enc_taps, enc_gain, own_keep[0], spread_matrix, enc_xhat, enc_rstd],
                [row_shape],
                *back_state,
                state,
                cols,
                enc_flops,
            )
            sent.append(send(y, level, level - 1) if level > 0 else y)
        current = sent
    enc_cot_all = lax.all_gather(state[1], "dp")
    enc_weight_out, enc_gain_out = weight_grad(enc_act_all, enc_cot_all, ENC_TAPS)
    return (enc_weight_out[None], enc_gain_out, dec_weight_out[None], dec_gain_out)


def solution(mesh):
    placed = (
        P("dp", None, None, None, None),
        P("dp"),
        P("dp"),
        P("dp", None, None, None, None),
        P("dp", None),
        P("section", None, None),
        P("section", None),
        P("section", None, None),
        P("section", None),
    )
    return jax.shard_map(
        body,
        mesh=mesh,
        in_specs=placed,
        out_specs=(
            P("section", "dp", None),
            P("section", "dp"),
            P("section", "dp", None),
            P("section", "dp"),
        ),
        check_vma=False,
    )
```

```python
import functools
import math

import jax
import jax.numpy as jnp
import numpy as np
from jax import lax
from jax.experimental import pallas as pl
from jax.experimental.pallas import tpu as pltpu
from jax.sharding import PartitionSpec as P

GROUPS = 32
ENC_TAPS = 9
DEC_TAPS = 3
KERNELS_OF_A_CHAIN = 32
PAIRS_APART = 4
BF16 = jnp.bfloat16
F32 = jnp.float32
VMEM_LIMIT = 32 * 1024 * 1024


def noise_level(timesteps):
    phase_arg = (timesteps.astype(F32) / 1000.0 + 0.008) / 1.008
    return jnp.cos(phase_arg * (math.pi / 2.0)) ** 2


def group_means(sums, spread_matrix, count, splits):
    rest = sums
    pieces = []
    for _ in range(splits - 1):
        piece = rest.astype(BF16).astype(F32)
        pieces.append(piece)
        rest = rest - piece
    pieces.append(rest)
    number = sums.shape[0]
    parts = jnp.concatenate(pieces, axis=0).astype(BF16)
    spread = jnp.dot(parts, spread_matrix, preferred_element_type=F32)
    total = spread[:number]
    for place in range(1, splits):
        total = total + spread[place * number : (place + 1) * number]
    folded = total.reshape(number // 8, 8, sums.shape[1])
    return jnp.sum(folded, axis=1, keepdims=True) * (1.0 / count)


def eight_rows(values):
    return jnp.sum(values.reshape(-1, 8, values.shape[-1]), axis=0)


def sigmoid(z):
    return 0.5 * jnp.tanh(0.5 * z) + 0.5


def spatial_shift(frames, row_offset, col_offset, height, width):
    step = row_offset * width + col_offset
    length = height * width
    moved = pltpu.roll(frames, (-step) % length, axis=1) if step % length else frames
    if row_offset == 0 and col_offset == 0:
        return moved
    place = lax.broadcasted_iota(jnp.int32, (1, length, 1), 1)
    row = place // width + row_offset
    col = place % width + col_offset
    inside = (row >= 0) & (row < height) & (col >= 0) & (col < width)
    return jnp.where(inside, moved, 0.0)


def spatial_columns_into(cols_ref, values_ref, sizes, sign):
    each = sizes.height * sizes.width
    pair = 2 * each
    channels = sizes.channels

    def one_pair(index, carry):
        place = pl.ds(pl.multiple_of(index * pair, pair), pair)
        frames = values_ref[place].reshape(2, each, channels)
        for tap in range(ENC_TAPS):
            moved = spatial_shift(
                frames, sign * (tap // 3 - 1), sign * (tap % 3 - 1), sizes.height, sizes.width
            )
            cols_ref[tap // 3, place, (tap % 3) * channels : (tap % 3 + 1) * channels] = (
                moved.reshape(pair, channels).astype(BF16)
            )
        return carry

    lax.fori_loop(0, sizes.rows // pair, one_pair, 0)


def temporal_pieces(values, frames, sign):
    samples, length, channels = values.shape
    each = length // frames
    blank = jnp.zeros((samples, each, channels), F32)
    before = jnp.concatenate([blank, values[:, : length - each]], axis=1)
    after = jnp.concatenate([values[:, each:], blank], axis=1)
    ordered = (before, values, after) if sign > 0 else (after, values, before)
    return [piece.reshape(samples * length, channels).astype(BF16) for piece in ordered]


def dot_nt(left, right):
    return lax.dot_general(left, right, (((1,), (1,)), ((), ())), preferred_element_type=F32)


class Sizes:
    def __init__(self, noise_draw, sections):
        self.micro, self.frames, self.height, self.width, self.channels = noise_draw.shape
        self.length = self.frames * self.height * self.width
        self.per_step = max(1, self.micro * sections // KERNELS_OF_A_CHAIN)
        self.steps = self.micro // self.per_step
        self.rows = self.per_step * self.length
        self.count = self.length * (self.channels // GROUPS)
        self.total = self.micro * self.length

    def sample(self, index):
        return slice(index * self.length, (index + 1) * self.length)


def norm_forward(sizes, values_ref, gain, spread_matrix, xhat_ref, rstd_ref):
    samples = range(sizes.per_step)
    sums = jnp.concatenate([eight_rows(values_ref[sizes.sample(s)]) for s in samples], axis=0)
    mean = group_means(sums, spread_matrix, sizes.count, 3)
    squares = []
    for s in samples:
        center = values_ref[sizes.sample(s)] - mean[s]
        values_ref[sizes.sample(s)] = center
        squares.append(eight_rows(center * center))
    spread = group_means(jnp.concatenate(squares, axis=0), spread_matrix, sizes.count, 3)
    rstd = lax.rsqrt(spread + 1e-05)
    for s in samples:
        normed = values_ref[sizes.sample(s)] * rstd[s]
        xhat_ref[sizes.sample(s)] = normed
        rstd_ref[s] = rstd[s]
        z = normed * gain
        values_ref[sizes.sample(s)] = z * sigmoid(z)


def residual(sizes, step, base_ref, keep_ref, branch_ref):
    out = []
    for s in range(sizes.per_step):
        index = step * sizes.per_step + s
        keep = keep_ref[index : index + 1]
        out.append(base_ref[sizes.sample(s)] + keep * branch_ref[sizes.sample(s)])
    return jnp.concatenate(out, axis=0)


def gate(sizes, step, keep_ref, values):
    out = []
    for s in range(sizes.per_step):
        index = step * sizes.per_step + s
        out.append(keep_ref[index : index + 1] * values[sizes.sample(s)])
    return jnp.concatenate(out, axis=0)


def started(source, target, sem):
    copy = pltpu.make_async_copy(source, target, sem)
    copy.start()
    return copy


def parts_of(sizes, step):
    return pl.ds(step * sizes.rows, sizes.rows), pl.ds(step * sizes.per_step, sizes.per_step)


def enc_forward_kernel(sizes, level, step, final, x_ref, w_ref, gain_ref, keep_ref, spread_ref, *refs):
    outs = refs[:-8]
    y_ref, xhat_far, rstd_far, act_far = outs[-4:] if final else outs[-5:-1]
    cols_ref, base_ref, values_ref, xhat_ref, rstd_ref, half_ref, sems = refs[-8:-1]
    out_ref = refs[-1]

    @pl.when(lax.axis_index("section") == level)
    def _():
        part, samples = parts_of(sizes, step)
        x = (x_ref[part] if level == 0 else x_ref[...]).astype(F32)
        base_ref[...] = x
        values_ref[...] = x
        norm_forward(
            sizes, values_ref, gain_ref[...], spread_ref[...], xhat_ref, rstd_ref
        )
        half_ref[...] = values_ref[...].astype(BF16)
        copies = [
            started(half_ref, act_far.at[part], sems.at[0]),
            started(xhat_ref, xhat_far.at[part], sems.at[1]),
            started(rstd_ref, rstd_far.at[samples], sems.at[2]),
        ]
        spatial_columns_into(cols_ref, values_ref, sizes, 1)

        def add_third(third, carry):
            part = jnp.dot(cols_ref[third], w_ref[third], preferred_element_type=F32)
            values_ref[...] = jnp.where(third == 0, part, values_ref[...] + part)
            return carry

        lax.fori_loop(0, 3, add_third, 0)
        out = residual(sizes, step, base_ref, keep_ref, values_ref).astype(BF16)
        y_ref[...] = out
        if not final:
            out_ref[...] = out
            copies.append(started(out_ref, outs[-1].at[part], sems.at[3]))
        for copy in copies:
            copy.wait()


def dec_forward_kernel(
    sizes, level, step, first, scale, x_ref, w_ref, gain_ref, keep_ref, spread_ref, *refs
):
    work = refs[-6:]
    base_ref, values_ref, xhat_ref, rstd_ref, half_ref, sems = work
    y_ref, xhat_far, rstd_far, act_far = refs[-10:-6]

    @pl.when(lax.axis_index("section") == level)
    def _():
        part, samples = parts_of(sizes, step)
        x = x_ref[...].astype(F32)
        base_ref[...] = x
        values_ref[...] = x + (x if first else refs[0][part].astype(F32))
        norm_forward(
            sizes, values_ref, gain_ref[...], spread_ref[...], xhat_ref, rstd_ref
        )
        half_ref[...] = values_ref[...].astype(BF16)
        copies = [
            started(half_ref, act_far.at[part], sems.at[0]),
            started(xhat_ref, xhat_far.at[part], sems.at[1]),
            started(rstd_ref, rstd_far.at[samples], sems.at[2]),
        ]
        act = values_ref[...].reshape(sizes.per_step, sizes.length, sizes.channels)
        columns = jnp.concatenate(temporal_pieces(act, sizes.frames, 1), axis=1)
        values_ref[...] = jnp.dot(columns, w_ref[...], preferred_element_type=F32)
        out = residual(sizes, step, base_ref, keep_ref, values_ref).astype(BF16)
        if scale is not None:
            noise = refs[0 if first else 1][part].astype(F32)
            out = ((out.astype(F32) - noise) * scale).astype(BF16)
        y_ref[...] = out
        for copy in copies:
            copy.wait()


def norm_back(sizes, cot_ref, gain, spread_matrix, xhat_ref, rstd_ref):
    samples = range(sizes.per_step)
    sums, products = [], []
    gain_rows = 0.0
    for s in samples:
        normed = xhat_ref[sizes.sample(s)]
        z = normed * gain
        sig = sigmoid(z)
        dz = cot_ref[sizes.sample(s)] * (sig * (1.0 + z * (1.0 - sig)))
        gain_rows = gain_rows + eight_rows(dz * normed)
        dn = dz * gain
        cot_ref[sizes.sample(s)] = dn
        sums.append(eight_rows(dn))
        products.append(eight_rows(dn * normed))
    means = group_means(jnp.concatenate(sums + products, axis=0), spread_matrix, sizes.count, 2)
    for s in samples:
        normed = xhat_ref[sizes.sample(s)]
        cot_ref[sizes.sample(s)] = rstd_ref[s] * (
            cot_ref[sizes.sample(s)] - means[s] - normed * means[sizes.per_step + s]
        )
    return gain_rows


def add_gain(sizes, step, gain_acc_ref, gain_rows, cot_far, half_ref, sem):
    total = gain_rows if step == 0 else gain_acc_ref[...] + gain_rows
    gain_acc_ref[...] = total
    if step == sizes.steps - 1:
        row = jnp.sum(total, axis=0, keepdims=True)
        tail = jnp.concatenate([row, jnp.zeros((15, sizes.channels), F32)], axis=0)
        half_ref[:16] = tail.astype(BF16)
        started(half_ref.at[pl.ds(0, 16)], cot_far.at[pl.ds(sizes.total, 16)], sem).wait()


def enc_backward_kernel(
    sizes, level, step, last, x_ref, w_ref, gain_ref, keep_ref, spread_ref, *refs
):
    xhat_far, rstd_far = refs[:2] if last else refs[1:3]
    cols_ref, base_ref, values_ref, xhat_ref, rstd_ref, half_ref, sems = refs[-7:]
    outs = refs[:-7]
    y_ref, gain_acc_ref, cot_far = outs[-3:]

    @pl.when(lax.axis_index("section") == level)
    def _():
        part, samples = parts_of(sizes, step)
        loads = [
            started(xhat_far.at[part], xhat_ref, sems.at[1]),
            started(rstd_far.at[samples], rstd_ref, sems.at[2]),
        ]
        t = x_ref[...]
        if not last:
            t = (t.astype(F32) + refs[0][part].astype(F32)).astype(BF16)
        t = t.astype(F32)
        base_ref[...] = t
        gated = gate(sizes, step, keep_ref, t)
        values_ref[...] = gated
        half_ref[...] = gated.astype(BF16)
        store = started(half_ref, cot_far.at[part], sems.at[0])
        spatial_columns_into(cols_ref, values_ref, sizes, -1)

        def add_third(third, carry):
            part = jnp.zeros((sizes.rows, sizes.channels), F32)
            for tap in range(3):
                where = slice(tap * sizes.channels, (tap + 1) * sizes.channels)
                part = part + dot_nt(cols_ref[third, :, where], w_ref[third, where, :])
            values_ref[...] = jnp.where(third == 0, part, values_ref[...] + part)
            return carry

        lax.fori_loop(0, 3, add_third, 0)
        for copy in loads:
            copy.wait()
        gain_rows = norm_back(
            sizes, values_ref, gain_ref[...], spread_ref[...], xhat_ref, rstd_ref
        )
        y_ref[...] = (base_ref[...] + values_ref[...]).astype(BF16)
        store.wait()
        add_gain(sizes, step, gain_acc_ref, gain_rows, cot_far, half_ref, sems.at[0])


def dec_backward_kernel(
    sizes, level, step, first, x_ref, w_ref, gain_ref, keep_ref, spread_ref, xhat_far, rstd_far, *refs
):
    base_ref, values_ref, xhat_ref, rstd_ref, half_ref, sems, skip_ref = refs[-7:]
    outs = refs[:-7]
    y_ref, gain_acc_ref, cot_far = outs[-3:] if first else outs[-4:-1]

    @pl.when(lax.axis_index("section") == level)
    def _():
        part, samples = parts_of(sizes, step)
        copies = [
            started(xhat_far.at[part], xhat_ref, sems.at[1]),
            started(rstd_far.at[samples], rstd_ref, sems.at[2]),
        ]
        g = x_ref[...].astype(F32)
        base_ref[...] = g
        gated = gate(sizes, step, keep_ref, g)
        half_ref[...] = gated.astype(BF16)
        store = started(half_ref, cot_far.at[part], sems.at[0])
        pieces = temporal_pieces(
            gated.reshape(sizes.per_step, sizes.length, sizes.channels), sizes.frames, -1
        )
        back = jnp.zeros((sizes.rows, sizes.channels), F32)
        for tap in range(DEC_TAPS):
            where = slice(tap * sizes.channels, (tap + 1) * sizes.channels)
            back = back + dot_nt(pieces[tap], w_ref[where, :])
        values_ref[...] = back
        for copy in copies:
            copy.wait()
        gain_rows = norm_back(
            sizes, values_ref, gain_ref[...], spread_ref[...], xhat_ref, rstd_ref
        )
        grad = values_ref[...]
        out = (base_ref[...] + grad).astype(BF16)
        skip_cot = grad.astype(BF16)
        if first:
            y_ref[...] = (out.astype(F32) + skip_cot.astype(F32)).astype(BF16)
        else:
            y_ref[...] = out
            skip_ref[...] = skip_cot
            started(skip_ref, outs[-1].at[part], sems.at[3]).wait()
        store.wait()
        add_gain(sizes, step, gain_acc_ref, gain_rows, cot_far, half_ref, sems.at[0])


def tap_span(rows_out, channels, taps, parts):
    span = 0
    for index in range(parts):
        start = index * rows_out
        span = max(span, -(-(start % channels + rows_out) // channels))
    return min(span, taps)


def weight_kernel(sizes, taps, span, rows_out, groups, *refs):
    act_ref, cot_refs = refs[0], refs[1 : groups + 1]
    out_ref, gain_out_ref, wide_ref = refs[-3:]
    me = lax.axis_index("dp")
    rows = groups * sizes.total
    base = jnp.minimum(me * rows_out // sizes.channels, taps - span)
    act = jnp.concatenate([act_ref[lax.rem(me + groups - by, groups)] for by in range(groups)], axis=0)
    act = act.astype(F32)
    cot = jnp.concatenate([ref[: sizes.total] for ref in cot_refs], axis=0)
    each = sizes.height * sizes.width
    gain = 0.0
    for ref in cot_refs:
        gain = gain + ref[sizes.total : sizes.total + 16].astype(F32)
    gain_out_ref[...] = gain[:8]
    for tap in range(taps):

        @pl.when((tap >= base) & (tap < base + span))
        def _(tap=tap):
            if taps == ENC_TAPS:
                frames = act.reshape(rows // each, each, sizes.channels)
                moved = spatial_shift(frames, tap // 3 - 1, tap % 3 - 1, sizes.height, sizes.width)
                moved = moved.reshape(rows, sizes.channels).astype(BF16)
            else:
                values = act.reshape(rows // sizes.length, sizes.length, sizes.channels)
                moved = temporal_pieces(values, sizes.frames, 1)[tap]
            place = pl.multiple_of((tap - base) * sizes.channels, sizes.channels)
            wide_ref[pl.ds(place, sizes.channels)] = lax.dot_general(
                moved, cot, (((0,), (0,)), ((), ())), preferred_element_type=F32
            )

    offset = pl.multiple_of(me * rows_out - base * sizes.channels, 16)
    out_ref[...] = wide_ref[pl.ds(offset, rows_out)]


def prologue_kernel(
    sizes,
    sections,
    ids_ref,
    times_ref,
    keep_ref,
    pool_ref,
    noise_ref,
    enc_ref,
    dec_ref,
    enc_out,
    dec_out,
    spread_out,
    start_out,
    enc_keep_out,
    dec_keep_out,
    sems,
):
    copies = [
        started(enc_ref, enc_out, sems.at[0]),
        started(dec_ref, dec_out, sems.at[1]),
    ]
    channels = sizes.channels
    own = lax.axis_index("section")
    row = lax.broadcasted_iota(jnp.int32, (sizes.micro, channels), 0)
    times = jnp.zeros((sizes.micro, channels), F32)
    enc_keep = jnp.zeros((sizes.micro, channels), F32)
    dec_keep = jnp.zeros((sizes.micro, channels), F32)
    for index in range(sizes.micro):
        here = row == index
        times = jnp.where(here, times_ref[index].astype(F32), times)
        enc_keep = jnp.where(here, keep_ref[index, own].astype(F32), enc_keep)
        dec_keep = jnp.where(here, keep_ref[index, own + sections].astype(F32), dec_keep)
    enc_keep_out[...] = enc_keep
    dec_keep_out[...] = dec_keep
    level = noise_level(times)
    clean_part, noise_part = jnp.sqrt(level), jnp.sqrt(1.0 - level)
    for first in range(0, sizes.micro, 2):
        place = slice(first * sizes.length, (first + 2) * sizes.length)
        noise = noise_ref[place].astype(F32)
        mixed = []
        for index in (first, first + 1):
            clean = pool_ref[ids_ref[index]].astype(F32)
            own_noise = noise[sizes.sample(index - first)]
            mixed.append(
                clean_part[index : index + 1] * clean + noise_part[index : index + 1] * own_noise
            )
        start_out[place] = jnp.concatenate(mixed, axis=0).astype(BF16)
    per_group = channels // GROUPS
    left = lax.broadcasted_iota(jnp.int32, (channels, channels), 0) // per_group
    right = lax.broadcasted_iota(jnp.int32, (channels, channels), 1) // per_group
    spread_out[...] = jnp.where(left == right, 1.0, 0.0).astype(BF16)
    for copy in copies:
        copy.wait()


VM = pl.BlockSpec(memory_space=pltpu.VMEM)
ANY = pl.BlockSpec(memory_space=pl.ANY)


def params():
    return pltpu.CompilerParams(vmem_limit_bytes=VMEM_LIMIT)


SM = pl.BlockSpec(memory_space=pltpu.SMEM)


def in_vmem(value):
    return pltpu.with_memory_space_constraint(value, pltpu.VMEM)


def staged_call(kernel, near, distant, plain_outs, kept, far, state, scratch, flops):
    state = list(state) if state is not None else [None] * (len(kept) + len(far))
    inputs = [in_vmem(value) for value in near] + list(distant)
    in_specs = [VM] * len(near) + [ANY] * len(distant)
    aliases = {}
    for place, value in enumerate(state):
        if value is None:
            continue
        aliases[len(inputs)] = len(plain_outs) + place
        close = place < len(kept)
        inputs.append(in_vmem(value) if close else value)
        in_specs.append(VM if close else ANY)
    outs = pl.pallas_call(
        kernel,
        in_specs=in_specs,
        out_specs=[VM] * (len(plain_outs) + len(kept)) + [ANY] * len(far),
        out_shape=[pltpu.VMEM(s, d) for s, d in list(plain_outs) + list(kept)]
        + [jax.ShapeDtypeStruct(s, d) for s, d in far],
        scratch_shapes=scratch,
        input_output_aliases=aliases,
        compiler_params=params(),
        cost_estimate=pl.CostEstimate(flops=flops, bytes_accessed=0, transcendentals=0),
    )(*inputs)
    return list(outs[: len(plain_outs)]), list(outs[len(plain_outs) :])


def body(
    clip_pool,
    sample_ids,
    timesteps,
    noise_draw,
    keep_lists,
    enc_weight,
    enc_gain,
    dec_weight,
    dec_gain,
):
    sections = lax.axis_size("section")
    parts = lax.axis_size("dp")
    sizes = Sizes(noise_draw, sections)
    channels, rows, steps, total_rows = sizes.channels, sizes.rows, sizes.steps, sizes.total
    scale = 1.0 / math.sqrt(sizes.micro * parts * sizes.length)
    last = sections - 1

    clips = clip_pool.reshape(clip_pool.shape[0], sizes.length, channels)
    noise = noise_draw.reshape(total_rows, channels)
    enc_taps = enc_weight.reshape(3, 3 * channels, channels)
    dec_taps = dec_weight.reshape(DEC_TAPS * channels, channels)
    enc_taps, dec_taps, spread_matrix, start, enc_keep, dec_keep = pl.pallas_call(
        functools.partial(prologue_kernel, sizes, sections),
        in_specs=[SM] * 3 + [VM] * 2 + [pl.BlockSpec(memory_space=pltpu.HBM)] * 2,
        out_specs=[VM] * 6,
        out_shape=[
            pltpu.VMEM(enc_taps.shape, BF16),
            pltpu.VMEM(dec_taps.shape, BF16),
            pltpu.VMEM((channels, channels), BF16),
            pltpu.VMEM(noise.shape, BF16),
            pltpu.VMEM((sizes.micro, channels), F32),
            pltpu.VMEM((sizes.micro, channels), F32),
        ],
        scratch_shapes=[pltpu.SemaphoreType.DMA((2,))],
        compiler_params=params(),
    )(
        sample_ids,
        timesteps,
        keep_lists,
        clips,
        noise,
        pltpu.with_memory_space_constraint(enc_taps, pltpu.HBM),
        pltpu.with_memory_space_constraint(dec_taps, pltpu.HBM),
    )

    row_shape = ((rows, channels), BF16)
    all_rows = ((total_rows, channels), BF16)
    forward_far = [((total_rows, channels), F32), ((sizes.micro, 1, channels), F32), all_rows]
    gain_kept = [((8, channels), F32)]
    cot_far = [((total_rows + 16, channels), BF16)]
    half = pltpu.VMEM((rows, channels), BF16)
    work = [
        pltpu.VMEM((rows, channels), F32),
        pltpu.VMEM((rows, channels), F32),
        pltpu.VMEM((rows, channels), F32),
        pltpu.VMEM((sizes.per_step, 1, channels), F32),
        half,
        pltpu.SemaphoreType.DMA((4,)),
    ]
    cols = [pltpu.VMEM((3, rows, 3 * channels), BF16)] + work
    enc_flops = 2 * rows * ENC_TAPS * channels * channels
    dec_flops = 2 * rows * DEC_TAPS * channels * channels

    def send(value, source, by):
        pairs = [
            (other, (other + by) % sections)
            for other in range(source % PAIRS_APART, sections, PAIRS_APART)
        ]
        return lax.ppermute(value, "section", pairs)

    def mirrored(value):
        return lax.ppermute(value, "section", [(i, last - i) for i in range(sections)])

    def gathered(value):
        others = [
            lax.ppermute(value, "dp", [(i, (i + by) % parts) for i in range(parts)])
            for by in range(1, parts)
        ]
        return [value] + others

    current = [start] * steps
    enc_state = None
    for level in range(sections):
        sent = []
        final = level == last
        if final:
            skip = mirrored(enc_state[3])
            enc_state = enc_state[:3]
        for step in range(steps):
            (y,), enc_state = staged_call(
                functools.partial(enc_forward_kernel, sizes, level, step, final),
                [current[step], enc_taps, enc_gain, enc_keep, spread_matrix],
                sent[:1] if level == last - 1 and step == steps - 1 and step > 0 else [],
                [row_shape],
                [],
                forward_far + ([] if final else [all_rows]),
                enc_state,
                cols + [half],
                enc_flops,
            )
            sent.append(send(y, level, 1))
        current = sent
    enc_xhat, enc_rstd, enc_act = enc_state
    enc_acts = lax.all_gather(enc_act, "dp")

    dec_state = None
    for level in range(sections):
        sent = []
        first, final = level == 0, level == last
        for step in range(steps):
            tied = [skip] if first and step == 0 else []
            near = [current[step], dec_taps, dec_gain, dec_keep, spread_matrix]
            near = near + ([] if first else [skip]) + ([noise] if final else [])
            (y,), dec_state = staged_call(
                functools.partial(
                    dec_forward_kernel, sizes, level, step, first, scale if final else None
                ),
                near,
                tied,
                [row_shape],
                [],
                forward_far,
                dec_state,
                work,
                dec_flops,
            )
            sent.append(y if final else send(y, level, 1))
        current = sent
    dec_xhat, dec_rstd, dec_act = dec_state
    dec_acts = lax.all_gather(dec_act, "dp")

    state = None
    for level in reversed(range(sections)):
        sent = []
        first = level == 0
        if first:
            skip = mirrored(state[2])
            state = state[:2]
        for step in range(steps):
            tied = sent[:1] if level == 1 and step == steps - 1 and step > 0 else []
            (y,), state = staged_call(
                functools.partial(dec_backward_kernel, sizes, level, step, first),
                [current[step], dec_taps, dec_gain, dec_keep, spread_matrix],
                [dec_xhat, dec_rstd] + tied,
                [row_shape],
                gain_kept,
                cot_far + ([] if first else [all_rows]),
                state,
                work + [half],
                dec_flops,
            )
            sent.append(send(y, level, -1))
        current = sent
    dec_cot = state[1]

    def weight_grad(acts, cots, taps):
        rows_out = taps * channels // parts
        span = tap_span(rows_out, channels, taps, parts)
        return pl.pallas_call(
            functools.partial(weight_kernel, sizes, taps, span, rows_out, parts),
            in_specs=[VM] * (1 + parts),
            out_specs=[VM, VM],
            out_shape=[
                jax.ShapeDtypeStruct((rows_out, channels), F32),
                jax.ShapeDtypeStruct((8, channels), F32),
            ],
            scratch_shapes=[pltpu.VMEM((span * channels, channels), F32)],
            compiler_params=params(),
            cost_estimate=pl.CostEstimate(
                flops=2 * span * channels * channels * parts * total_rows,
                bytes_accessed=rows_out * channels * 4,
                transcendentals=0,
            ),
        )(*[in_vmem(value) for value in [acts] + cots])

    def own_gain(gain):
        width = channels // parts
        return lax.dynamic_slice(gain, (0, lax.axis_index("dp") * width), (1, width))

    dec_weight_out, dec_gain_out = weight_grad(dec_acts, gathered(dec_cot), DEC_TAPS)

    state = None
    for level in reversed(range(sections)):
        sent = []
        final = level == last
        for step in range(steps):
            near = [current[step], enc_taps, enc_gain, enc_keep, spread_matrix]
            near = near + ([] if final else [skip])
            distant = [enc_xhat, enc_rstd]
            tied = []
            if step == 0 and level >= last - 1:
                tied = [skip] if final else [dec_gain_out]
            (y,), state = staged_call(
                functools.partial(enc_backward_kernel, sizes, level, step, final),
                near,
                distant + tied,
                [row_shape],
                gain_kept,
                cot_far,
                state,
                cols,
                enc_flops,
            )
            sent.append(send(y, level, -1) if level > 0 else y)
        current = sent
    enc_weight_out, enc_gain_out = weight_grad(enc_acts, gathered(state[1]), ENC_TAPS)
    return (
        enc_weight_out[None],
        own_gain(enc_gain_out),
        dec_weight_out[None],
        own_gain(dec_gain_out),
    )


def solution(mesh):
    placed = (
        P("dp", None, None, None, None),
        P("dp"),
        P("dp"),
        P("dp", None, None, None, None),
        P("dp", None),
        P("section", None, None),
        P("section", None),
        P("section", None, None),
        P("section", None),
    )
    return jax.shard_map(
        body,
        mesh=mesh,
        in_specs=placed,
        out_specs=(
            P("section", "dp", None),
            P("section", "dp"),
            P("section", "dp", None),
            P("section", "dp"),
        ),
        check_vma=False,
    )
```

```python
import functools
import math

import jax
import jax.numpy as jnp
import numpy as np
from jax import lax
from jax.experimental import pallas as pl
from jax.experimental.pallas import tpu as pltpu
from jax.sharding import PartitionSpec as P

GROUPS = 32
ENC_TAPS = 9
DEC_TAPS = 3
KERNELS_OF_A_CHAIN = 32
PAIRS_APART = 3
LAG = 3
LAG_BESIDE = 2
BF16 = jnp.bfloat16
F32 = jnp.float32
VMEM_LIMIT = 32 * 1024 * 1024


def noise_level(timesteps):
    phase_arg = (timesteps.astype(F32) / 1000.0 + 0.008) / 1.008
    return jnp.cos(phase_arg * (math.pi / 2.0)) ** 2


def group_means(sums, spread_matrix, count, splits):
    rest = sums
    pieces = []
    for _ in range(splits - 1):
        piece = rest.astype(BF16).astype(F32)
        pieces.append(piece)
        rest = rest - piece
    pieces.append(rest)
    number = sums.shape[0]
    parts = jnp.concatenate(pieces, axis=0).astype(BF16)
    spread = jnp.dot(parts, spread_matrix, preferred_element_type=F32)
    total = spread[:number]
    for place in range(1, splits):
        total = total + spread[place * number : (place + 1) * number]
    folded = total.reshape(number // 8, 8, sums.shape[1])
    return jnp.sum(folded, axis=1, keepdims=True) * (1.0 / count)


def eight_rows(values):
    return jnp.sum(values.reshape(-1, 8, values.shape[-1]), axis=0)


def sigmoid(z):
    return 0.5 * jnp.tanh(0.5 * z) + 0.5


def spatial_shift(frames, row_offset, col_offset, height, width):
    step = row_offset * width + col_offset
    length = height * width
    moved = pltpu.roll(frames, (-step) % length, axis=1) if step % length else frames
    if row_offset == 0 and col_offset == 0:
        return moved
    place = lax.broadcasted_iota(jnp.int32, (1, length, 1), 1)
    row = place // width + row_offset
    col = place % width + col_offset
    inside = (row >= 0) & (row < height) & (col >= 0) & (col < width)
    return jnp.where(inside, moved, 0.0)


def spatial_columns_into(cols_ref, values_ref, sizes, sign):
    each = sizes.height * sizes.width
    pair = 2 * each
    channels = sizes.channels

    def one_pair(index, carry):
        place = pl.ds(pl.multiple_of(index * pair, pair), pair)
        frames = values_ref[place].reshape(2, each, channels)
        for tap in range(ENC_TAPS):
            moved = spatial_shift(
                frames, sign * (tap // 3 - 1), sign * (tap % 3 - 1), sizes.height, sizes.width
            )
            cols_ref[tap // 3, place, (tap % 3) * channels : (tap % 3 + 1) * channels] = (
                moved.reshape(pair, channels).astype(BF16)
            )
        return carry

    lax.fori_loop(0, sizes.rows // pair, one_pair, 0)


def temporal_pieces(values, frames, sign):
    samples, length, channels = values.shape
    each = length // frames
    blank = jnp.zeros((samples, each, channels), F32)
    before = jnp.concatenate([blank, values[:, : length - each]], axis=1)
    after = jnp.concatenate([values[:, each:], blank], axis=1)
    ordered = (before, values, after) if sign > 0 else (after, values, before)
    return [piece.reshape(samples * length, channels).astype(BF16) for piece in ordered]


def dot_nt(left, right):
    return lax.dot_general(left, right, (((1,), (1,)), ((), ())), preferred_element_type=F32)


class Sizes:
    def __init__(self, noise_draw, sections):
        self.micro, self.frames, self.height, self.width, self.channels = noise_draw.shape
        self.length = self.frames * self.height * self.width
        self.per_step = max(1, self.micro * sections // KERNELS_OF_A_CHAIN)
        self.steps = self.micro // self.per_step
        self.rows = self.per_step * self.length
        self.count = self.length * (self.channels // GROUPS)
        self.total = self.micro * self.length

    def split(self, level, step):
        return level > 0 or step < self.steps // 2

    def sample(self, index):
        return slice(index * self.length, (index + 1) * self.length)


def norm_forward(sizes, values_ref, gain, spread_matrix, xhat_ref, rstd_ref):
    samples = range(sizes.per_step)
    sums = jnp.concatenate([eight_rows(values_ref[sizes.sample(s)]) for s in samples], axis=0)
    mean = group_means(sums, spread_matrix, sizes.count, 3)
    squares = []
    for s in samples:
        center = values_ref[sizes.sample(s)] - mean[s]
        values_ref[sizes.sample(s)] = center
        squares.append(eight_rows(center * center))
    spread = group_means(jnp.concatenate(squares, axis=0), spread_matrix, sizes.count, 3)
    rstd = lax.rsqrt(spread + 1e-05)
    for s in samples:
        normed = values_ref[sizes.sample(s)] * rstd[s]
        xhat_ref[sizes.sample(s)] = normed
        rstd_ref[s] = rstd[s]
        z = normed * gain
        values_ref[sizes.sample(s)] = z * sigmoid(z)


def residual(sizes, step, base_ref, keep_ref, branch_ref):
    out = []
    for s in range(sizes.per_step):
        index = step * sizes.per_step + s
        keep = keep_ref[index : index + 1]
        out.append(base_ref[sizes.sample(s)] + keep * branch_ref[sizes.sample(s)])
    return jnp.concatenate(out, axis=0)


def gate(sizes, step, keep_ref, values):
    out = []
    for s in range(sizes.per_step):
        index = step * sizes.per_step + s
        out.append(keep_ref[index : index + 1] * values[sizes.sample(s)])
    return jnp.concatenate(out, axis=0)


def started(source, target, sem):
    copy = pltpu.make_async_copy(source, target, sem)
    copy.start()
    return copy


def parts_of(sizes, step):
    return pl.ds(step * sizes.rows, sizes.rows), pl.ds(step * sizes.per_step, sizes.per_step)


def store_norms(sizes, step, xhat_ref, rstd_ref, half_ref, xhat_far, rstd_far, bulk_far, first_row, sems):
    part, samples = parts_of(sizes, step)
    place = pl.ds(first_row + step * sizes.rows, sizes.rows)
    return [
        started(half_ref, bulk_far.at[place], sems.at[0]),
        started(xhat_ref, xhat_far.at[part], sems.at[1]),
        started(rstd_ref, rstd_far.at[samples], sems.at[2]),
    ]


def enc_forward_kernel(sizes, level, step, final, x_ref, w_ref, gain_ref, keep_ref, spread_ref, *refs):
    y_ref, out_ref, xhat_far, rstd_far, bulk_far = refs[-12:-7]
    cols_ref, base_ref, values_ref, xhat_ref, rstd_ref, half_ref, sems = refs[-7:]

    @pl.when(lax.axis_index("section") == level)
    def _():
        part, _ = parts_of(sizes, step)
        x = (x_ref[part] if level == 0 else x_ref[...]).astype(F32)
        base_ref[...] = x
        values_ref[...] = x
        norm_forward(
            sizes, values_ref, gain_ref[...], spread_ref[...], xhat_ref, rstd_ref
        )
        half_ref[...] = values_ref[...].astype(BF16)
        copies = store_norms(
            sizes, step, xhat_ref, rstd_ref, half_ref, xhat_far, rstd_far, bulk_far, 0, sems
        )
        spatial_columns_into(cols_ref, values_ref, sizes, 1)

        def add_third(third, carry):
            part = jnp.dot(cols_ref[third], w_ref[third], preferred_element_type=F32)
            values_ref[...] = jnp.where(third == 0, part, values_ref[...] + part)
            return carry

        lax.fori_loop(0, 3, add_third, 0)
        out = residual(sizes, step, base_ref, keep_ref, values_ref).astype(BF16)
        y_ref[...] = out
        if not final:
            out_ref[part] = out
        for copy in copies:
            copy.wait()


def dec_forward_kernel(
    sizes, home, step, first, scale, x_ref, w_ref, gain_ref, keep_ref, spread_ref, skip_ref, *refs
):
    base_ref, values_ref, xhat_ref, rstd_ref, half_ref, sems = refs[-6:]
    y_ref, xhat_far, rstd_far, bulk_far = refs[-10:-6]

    @pl.when(lax.axis_index("section") == home)
    def _():
        part, _ = parts_of(sizes, step)
        x = x_ref[...].astype(F32)
        base_ref[...] = x
        values_ref[...] = x + (x if first else skip_ref[part].astype(F32))
        norm_forward(
            sizes, values_ref, gain_ref[...], spread_ref[...], xhat_ref, rstd_ref
        )
        half_ref[...] = values_ref[...].astype(BF16)
        copies = store_norms(
            sizes, step, xhat_ref, rstd_ref, half_ref, xhat_far, rstd_far, bulk_far, sizes.total, sems
        )
        act = values_ref[...].reshape(sizes.per_step, sizes.length, sizes.channels)
        columns = jnp.concatenate(temporal_pieces(act, sizes.frames, 1), axis=1)
        values_ref[...] = jnp.dot(columns, w_ref[...], preferred_element_type=F32)
        out = residual(sizes, step, base_ref, keep_ref, values_ref).astype(BF16)
        if scale is not None:
            noise = refs[0][part].astype(F32)
            out = ((out.astype(F32) - noise) * scale).astype(BF16)
        y_ref[...] = out
        for copy in copies:
            copy.wait()


def norm_back(sizes, cot_ref, gain, spread_matrix, xhat_ref, rstd_ref):
    samples = range(sizes.per_step)
    sums, products = [], []
    gain_rows = 0.0
    for s in samples:
        normed = xhat_ref[sizes.sample(s)]
        z = normed * gain
        sig = sigmoid(z)
        dz = cot_ref[sizes.sample(s)] * (sig * (1.0 + z * (1.0 - sig)))
        gain_rows = gain_rows + eight_rows(dz * normed)
        dn = dz * gain
        cot_ref[sizes.sample(s)] = dn
        sums.append(eight_rows(dn))
        products.append(eight_rows(dn * normed))
    means = group_means(jnp.concatenate(sums + products, axis=0), spread_matrix, sizes.count, 2)
    for s in samples:
        normed = xhat_ref[sizes.sample(s)]
        cot_ref[sizes.sample(s)] = rstd_ref[s] * (
            cot_ref[sizes.sample(s)] - means[s] - normed * means[sizes.per_step + s]
        )
    return gain_rows


def add_gain(sizes, step, gain_acc_ref, gain_rows, cot_far, first_row, half_ref, sem):
    total = gain_rows if step == 0 else gain_acc_ref[...] + gain_rows
    gain_acc_ref[...] = total
    if step == sizes.steps - 1:
        row = jnp.sum(total, axis=0, keepdims=True)
        tail = jnp.concatenate([row, jnp.zeros((15, sizes.channels), F32)], axis=0)
        half_ref[:16] = tail.astype(BF16)
        started(half_ref.at[pl.ds(0, 16)], cot_far.at[pl.ds(first_row, 16)], sem).wait()


def enc_backward_kernel(
    sizes, level, step, last, x_ref, w_ref, gain_ref, keep_ref, spread_ref, *refs
):
    xhat_far, rstd_far = refs[:2] if last else refs[1:3]
    cols_ref, base_ref, values_ref, xhat_ref, rstd_ref, half_ref, sems = refs[-7:]
    outs = refs[-11:-7] if sizes.split(level, step) else refs[-10:-7]
    y_ref, gain_acc_ref = outs[:2]
    late = step >= sizes.steps // 2
    cot_far = outs[-1] if late else outs[2]
    first_row = (step - (sizes.steps // 2 if late else 0)) * sizes.rows

    @pl.when(lax.axis_index("section") == level)
    def _():
        part, samples = parts_of(sizes, step)
        loads = [
            started(xhat_far.at[part], xhat_ref, sems.at[1]),
            started(rstd_far.at[samples], rstd_ref, sems.at[2]),
        ]
        t = x_ref[...]
        if not last:
            t = (t.astype(F32) + refs[0][part].astype(F32)).astype(BF16)
        t = t.astype(F32)
        base_ref[...] = t
        gated = gate(sizes, step, keep_ref, t)
        values_ref[...] = gated
        half_ref[...] = gated.astype(BF16)
        store = started(half_ref, cot_far.at[pl.ds(first_row, sizes.rows)], sems.at[0])
        spatial_columns_into(cols_ref, values_ref, sizes, -1)

        def add_third(third, carry):
            part = jnp.zeros((sizes.rows, sizes.channels), F32)
            for tap in range(3):
                where = slice(tap * sizes.channels, (tap + 1) * sizes.channels)
                part = part + dot_nt(cols_ref[third, :, where], w_ref[third, where, :])
            values_ref[...] = jnp.where(third == 0, part, values_ref[...] + part)
            return carry

        lax.fori_loop(0, 3, add_third, 0)
        for copy in loads:
            copy.wait()
        gain_rows = norm_back(
            sizes, values_ref, gain_ref[...], spread_ref[...], xhat_ref, rstd_ref
        )
        y_ref[...] = (base_ref[...] + values_ref[...]).astype(BF16)
        store.wait()
        rows = (sizes.steps - sizes.steps // 2) * sizes.rows
        add_gain(sizes, step, gain_acc_ref, gain_rows, cot_far, rows, half_ref, sems.at[0])


def dec_backward_kernel(
    sizes, home, step, first, x_ref, w_ref, gain_ref, keep_ref, spread_ref, xhat_far, rstd_far, *refs
):
    base_ref, values_ref, xhat_ref, rstd_ref, half_ref, sems = refs[-6:]
    outs = refs[:-6]
    y_ref, gain_acc_ref = outs[-3:-1] if first else outs[-4:-2]
    bulk_far = outs[-1]

    @pl.when(lax.axis_index("section") == home)
    def _():
        part, samples = parts_of(sizes, step)
        copies = [
            started(xhat_far.at[part], xhat_ref, sems.at[1]),
            started(rstd_far.at[samples], rstd_ref, sems.at[2]),
        ]
        g = x_ref[...].astype(F32)
        base_ref[...] = g
        gated = gate(sizes, step, keep_ref, g)
        half_ref[...] = gated.astype(BF16)
        place = pl.ds(2 * sizes.total + step * sizes.rows, sizes.rows)
        store = started(half_ref, bulk_far.at[place], sems.at[0])
        pieces = temporal_pieces(
            gated.reshape(sizes.per_step, sizes.length, sizes.channels), sizes.frames, -1
        )
        back = jnp.zeros((sizes.rows, sizes.channels), F32)
        for tap in range(DEC_TAPS):
            where = slice(tap * sizes.channels, (tap + 1) * sizes.channels)
            back = back + dot_nt(pieces[tap], w_ref[where, :])
        values_ref[...] = back
        for copy in copies:
            copy.wait()
        gain_rows = norm_back(
            sizes, values_ref, gain_ref[...], spread_ref[...], xhat_ref, rstd_ref
        )
        grad = values_ref[...]
        out = (base_ref[...] + grad).astype(BF16)
        skip_cot = grad.astype(BF16)
        if first:
            y_ref[...] = (out.astype(F32) + skip_cot.astype(F32)).astype(BF16)
        else:
            y_ref[...] = out
            outs[-2][part] = skip_cot
        store.wait()
        add_gain(
            sizes, step, gain_acc_ref, gain_rows, bulk_far, 3 * sizes.total, half_ref, sems.at[0]
        )


def tap_span(rows_out, channels, taps, parts):
    span = 0
    for index in range(parts):
        start = index * rows_out
        span = max(span, -(-(start % channels + rows_out) // channels))
    return min(span, taps)


def tap_products(sizes, taps, span, rows_out, act, cot, wide_ref):
    me = lax.axis_index("dp")
    rows = act.shape[0]
    base = jnp.minimum(me * rows_out // sizes.channels, taps - span)
    each = sizes.height * sizes.width
    for tap in range(taps):

        @pl.when((tap >= base) & (tap < base + span))
        def _(tap=tap):
            if taps == ENC_TAPS:
                frames = act.reshape(rows // each, each, sizes.channels)
                moved = spatial_shift(frames, tap // 3 - 1, tap % 3 - 1, sizes.height, sizes.width)
                moved = moved.reshape(rows, sizes.channels).astype(BF16)
            else:
                values = act.reshape(rows // sizes.length, sizes.length, sizes.channels)
                moved = temporal_pieces(values, sizes.frames, 1)[tap]
            place = pl.multiple_of((tap - base) * sizes.channels, sizes.channels)
            wide_ref[pl.ds(place, sizes.channels)] = lax.dot_general(
                moved, cot, (((0,), (0,)), ((), ())), preferred_element_type=F32
            )

    offset = pl.multiple_of(me * rows_out - base * sizes.channels, 16)
    return wide_ref[pl.ds(offset, rows_out)]


def gain_sum(pieces):
    total = 0.0
    for piece in pieces:
        total = total + piece.astype(F32)
    return total


def dec_weight_kernel(sizes, span, rows_out, *refs):
    bulk_refs, out_ref, wide_ref = refs[:-2], refs[-2], refs[-1]
    total = sizes.total
    act = jnp.concatenate([ref[total : 2 * total] for ref in bulk_refs], axis=0).astype(F32)
    cot = jnp.concatenate([ref[2 * total : 3 * total] for ref in bulk_refs], axis=0)
    out_ref[:rows_out] = tap_products(
        sizes, DEC_TAPS, span, rows_out, act, cot, wide_ref
    ).astype(BF16)
    out_ref[rows_out : rows_out + 16] = gain_sum(
        [ref[3 * total : 3 * total + 16] for ref in bulk_refs]
    ).astype(BF16)


def own_lanes(parts, out_ref, row):
    width = row.shape[1] // parts
    for index in range(parts):

        @pl.when(lax.axis_index("dp") == index)
        def _(index=index):
            out_ref[...] = row[:, index * width : (index + 1) * width]


def enc_weight_kernel(sizes, span, rows_out, parts, *refs):
    bulk_refs, early_refs, late_refs = refs[:parts], refs[parts : 2 * parts], refs[2 * parts : 3 * parts]
    dec_ref, out_ref, gain_ref, dec_out_ref, dec_gain_ref, wide_ref = refs[3 * parts :]
    act = jnp.concatenate([ref[: sizes.total] for ref in bulk_refs], axis=0).astype(F32)
    pieces = []
    late_rows = late_refs[0].shape[0] - 16
    for early, late in zip(early_refs, late_refs):
        pieces.extend([early[...], late[:late_rows]])
    cot = jnp.concatenate(pieces, axis=0)
    own_lanes(parts, gain_ref, gain_sum([late[late_rows:] for late in late_refs])[:1])
    dec_rows = dec_out_ref.shape[0]
    dec_out_ref[...] = dec_ref[:dec_rows].astype(F32)
    own_lanes(parts, dec_gain_ref, dec_ref[dec_rows : dec_rows + 16].astype(F32)[:1])
    out_ref[...] = tap_products(sizes, ENC_TAPS, span, rows_out, act, cot, wide_ref)


def prologue_kernel(
    sizes,
    sections,
    ids_far,
    times_far,
    keep_far,
    pool_ref,
    noise_ref,
    dec_gain_ref,
    enc_ref,
    dec_ref,
    enc_out,
    spread_out,
    start_out,
    enc_keep_out,
    dec_keep_out,
    half_out,
    ids_ref,
    times_ref,
    keep_ref,
    gain_rows_ref,
    sems,
):
    half = half_out.shape[0] - 16
    rest = dec_gain_ref[...]
    gain_rows = []
    for _ in range(3):
        piece = rest.astype(BF16).astype(F32)
        gain_rows.append(piece)
        rest = rest - piece
    gain_rows.append(jnp.zeros((13, rest.shape[1]), F32))
    gain_rows_ref[...] = jnp.concatenate(gain_rows, axis=0).astype(BF16)
    core = lax.rem(lax.axis_index("dp"), 2)
    small = [
        started(ids_far, ids_ref, sems.at[2]),
        started(times_far, times_ref, sems.at[3]),
        started(keep_far, keep_ref, sems.at[4]),
    ]
    copies = [
        started(enc_ref, enc_out, sems.at[0]),
        started(
            dec_ref.at[pl.ds(pl.multiple_of(core * half, 16), half)],
            half_out.at[pl.ds(0, half)],
            sems.at[1],
        ),
        started(gain_rows_ref, half_out.at[pl.ds(half, 16)], sems.at[5]),
    ]
    channels = sizes.channels
    per_group = channels // GROUPS
    left = lax.broadcasted_iota(jnp.int32, (channels, channels), 0) // per_group
    right = lax.broadcasted_iota(jnp.int32, (channels, channels), 1) // per_group
    spread_out[...] = jnp.where(left == right, 1.0, 0.0).astype(BF16)
    for copy in small:
        copy.wait()
    own = lax.axis_index("section")
    row = lax.broadcasted_iota(jnp.int32, (sizes.micro, channels), 0)
    times = jnp.zeros((sizes.micro, channels), F32)
    enc_keep = jnp.zeros((sizes.micro, channels), F32)
    dec_keep = jnp.zeros((sizes.micro, channels), F32)
    for index in range(sizes.micro):
        here = row == index
        times = jnp.where(here, times_ref[index].astype(F32), times)
        enc_keep = jnp.where(here, keep_ref[index, own].astype(F32), enc_keep)
        dec_keep = jnp.where(here, keep_ref[index, 2 * sections - 1 - own].astype(F32), dec_keep)
    enc_keep_out[...] = enc_keep
    dec_keep_out[...] = dec_keep
    level = noise_level(times)
    clean_part, noise_part = jnp.sqrt(level), jnp.sqrt(1.0 - level)
    for first in range(0, sizes.micro, 2):
        place = slice(first * sizes.length, (first + 2) * sizes.length)
        noise = noise_ref[place].astype(F32)
        mixed = []
        for index in (first, first + 1):
            clean = pool_ref[ids_ref[index]].astype(F32)
            own_noise = noise[sizes.sample(index - first)]
            mixed.append(
                clean_part[index : index + 1] * clean + noise_part[index : index + 1] * own_noise
            )
        start_out[place] = jnp.concatenate(mixed, axis=0).astype(BF16)
    for copy in copies:
        copy.wait()


def join_kernel(own_far, other_far, out_ref, gain_ref, rows_ref, sems):
    half = own_far.shape[0] - 16
    core = lax.rem(lax.axis_index("dp"), 2)
    copies = [
        started(
            far.at[pl.ds(0, half)],
            out_ref.at[pl.ds(pl.multiple_of(place * half, 16), half)],
            sems.at[index],
        )
        for index, (far, place) in enumerate([(own_far, core), (other_far, 1 - core)])
    ]
    copies.append(started(own_far.at[pl.ds(half, 16)], rows_ref, sems.at[2]))
    for copy in copies:
        copy.wait()
    rows = rows_ref[...].astype(F32)
    gain_ref[...] = rows[0:1] + rows[1:2] + rows[2:3]


def passing(kernel, scratch_count):
    def run(*refs):
        cut = len(refs) - scratch_count - 1
        kernel(*refs[:cut], *refs[cut + 1 :])

    return run


VM = pl.BlockSpec(memory_space=pltpu.VMEM)
ANY = pl.BlockSpec(memory_space=pl.ANY)


def params():
    return pltpu.CompilerParams(vmem_limit_bytes=VMEM_LIMIT)


def in_vmem(value):
    return pltpu.with_memory_space_constraint(value, pltpu.VMEM)


def staged_call(kernel, near, distant, plain_outs, kept, far, state, scratch, flops):
    state = list(state) if state is not None else [None] * (len(kept) + len(far))
    inputs = [in_vmem(value) for value in near] + list(distant)
    in_specs = [VM] * len(near) + [ANY] * len(distant)
    aliases = {}
    for place, value in enumerate(state):
        if value is None:
            continue
        aliases[len(inputs)] = len(plain_outs) + place
        close = place < len(kept)
        inputs.append(in_vmem(value) if close else value)
        in_specs.append(VM if close else ANY)
    outs = pl.pallas_call(
        kernel,
        in_specs=in_specs,
        out_specs=[VM] * (len(plain_outs) + len(kept)) + [ANY] * len(far),
        out_shape=[pltpu.VMEM(s, d) for s, d in list(plain_outs) + list(kept)]
        + [jax.ShapeDtypeStruct(s, d) for s, d in far],
        scratch_shapes=scratch,
        input_output_aliases=aliases,
        compiler_params=params(),
        cost_estimate=pl.CostEstimate(flops=flops, bytes_accessed=0, transcendentals=0),
    )(*inputs)
    return list(outs[: len(plain_outs)]), list(outs[len(plain_outs) :])


def body(
    clip_pool,
    sample_ids,
    timesteps,
    noise_draw,
    keep_lists,
    enc_weight,
    enc_gain,
    dec_weight,
    dec_gain,
):
    sections = lax.axis_size("section")
    parts = lax.axis_size("dp")
    sizes = Sizes(noise_draw, sections)
    channels, rows, steps, total_rows = sizes.channels, sizes.rows, sizes.steps, sizes.total
    scale = 1.0 / math.sqrt(sizes.micro * parts * sizes.length)
    last = sections - 1

    def send(value, source, by):
        pairs = [
            (other, other + by)
            for other in range(source % PAIRS_APART, sections, PAIRS_APART)
            if 0 <= other + by < sections
        ]
        return lax.ppermute(value, "section", pairs)

    def mirrored(value):
        return lax.ppermute(value, "section", [(i, last - i) for i in range(sections)])

    def swapped(value, apart):
        return lax.ppermute(value, "dp", [(i, i ^ apart) for i in range(parts)])

    moves = []
    distances = [0]
    apart = parts // 2
    while apart:
        moves += [(place, apart) for place in range(len(distances))]
        distances += [distance ^ apart for distance in distances]
        apart //= 2

    clips = clip_pool.reshape(clip_pool.shape[0], sizes.length, channels)
    noise = noise_draw.reshape(total_rows, channels)
    enc_taps = enc_weight.reshape(3, 3 * channels, channels)
    dec_taps = dec_weight.reshape(DEC_TAPS * channels, channels)
    half_rows = DEC_TAPS * channels // 2
    enc_taps, spread_matrix, start, enc_keep, dec_keep, dec_half = pl.pallas_call(
        functools.partial(prologue_kernel, sizes, sections),
        in_specs=[ANY] * 3 + [VM] * 3 + [pl.BlockSpec(memory_space=pltpu.HBM)] * 2,
        out_specs=[VM] * 5 + [ANY],
        out_shape=[
            pltpu.VMEM(enc_taps.shape, BF16),
            pltpu.VMEM((channels, channels), BF16),
            pltpu.VMEM(noise.shape, BF16),
            pltpu.VMEM((sizes.micro, channels), F32),
            pltpu.VMEM((sizes.micro, channels), F32),
            jax.ShapeDtypeStruct((half_rows + 16, channels), BF16),
        ],
        scratch_shapes=[
            pltpu.SMEM(sample_ids.shape, jnp.int32),
            pltpu.SMEM(timesteps.shape, jnp.int32),
            pltpu.SMEM(keep_lists.shape, jnp.int32),
            pltpu.VMEM((16, channels), BF16),
            pltpu.SemaphoreType.DMA((6,)),
        ],
        compiler_params=params(),
    )(
        sample_ids,
        timesteps,
        keep_lists,
        clips,
        noise,
        dec_gain,
        pltpu.with_memory_space_constraint(enc_taps, pltpu.HBM),
        pltpu.with_memory_space_constraint(dec_taps, pltpu.HBM),
    )
    came = mirrored(dec_half)

    row_shape = ((rows, channels), BF16)
    all_rows = ((total_rows, channels), BF16)
    bulk_shape = ((3 * total_rows + 16, channels), BF16)
    norm_far = [((total_rows, channels), F32), ((sizes.micro, 1, channels), F32)]
    gain_kept = ((8, channels), F32)
    early_rows = (steps // 2) * rows
    early_shape = ((early_rows, channels), BF16)
    late_shape = ((total_rows - early_rows + 16, channels), BF16)
    work = [
        pltpu.VMEM((rows, channels), F32),
        pltpu.VMEM((rows, channels), F32),
        pltpu.VMEM((rows, channels), F32),
        pltpu.VMEM((sizes.per_step, 1, channels), F32),
        pltpu.VMEM((rows, channels), BF16),
        pltpu.SemaphoreType.DMA((3,)),
    ]
    cols = [pltpu.VMEM((3, rows, 3 * channels), BF16)] + work
    enc_flops = 2 * rows * ENC_TAPS * channels * channels
    dec_flops = 2 * rows * DEC_TAPS * channels * channels
    enc_consts = [enc_taps, enc_gain, enc_keep, spread_matrix]
    dec_consts = []
    held = dict.fromkeys(
        ["out", "enc_xhat", "enc_rstd", "dec_xhat", "dec_rstd", "bulk"]
        + ["dec_gain", "skip", "enc_gain", "early", "late"]
    )
    held["passed"] = None

    def stage(kernel, near, distant, kept, far, scratch, flops, passed=None):
        if passed is not None:
            held["passed"] = passed
            far = far + [("passed", (passed.shape, passed.dtype))]
            kernel = passing(kernel, len(scratch))
        names = [name for name, _ in kept + far]
        (y,), state = staged_call(
            kernel,
            near,
            distant,
            [row_shape],
            [shape for _, shape in kept],
            [shape for _, shape in far],
            [held[name] for name in names],
            scratch,
            flops,
        )
        held.update(zip(names, state))
        return y

    def enc_forward(level, step, x, tied, passed):
        return stage(
            functools.partial(enc_forward_kernel, sizes, level, step, level == last),
            [x] + enc_consts,
            tied,
            [("out", all_rows)],
            [("enc_xhat", norm_far[0]), ("enc_rstd", norm_far[1]), ("bulk", bulk_shape)],
            cols,
            enc_flops,
            passed,
        )

    def dec_forward(level, step, x, tied, passed):
        final = level == last
        return stage(
            functools.partial(
                dec_forward_kernel, sizes, last - level, step, level == 0, scale if final else None
            ),
            [x] + dec_consts + [held["out"]] + ([noise] if final else []),
            tied,
            [],
            [("dec_xhat", norm_far[0]), ("dec_rstd", norm_far[1]), ("bulk", bulk_shape)],
            work,
            dec_flops,
            passed,
        )

    def dec_backward(level, step, g, tied, passed):
        return stage(
            functools.partial(dec_backward_kernel, sizes, last - level, step, level == 0),
            [g] + dec_consts,
            [held["dec_xhat"], held["dec_rstd"]] + tied,
            [("dec_gain", gain_kept)] + ([("skip", all_rows)] if level > 0 else []),
            [("bulk", bulk_shape)],
            work,
            dec_flops,
            passed,
        )

    def enc_backward(level, step, t, tied, passed):
        final = level == last
        early = [("early", early_shape)] if sizes.split(level, step) else []
        return stage(
            functools.partial(enc_backward_kernel, sizes, level, step, final),
            [t] + enc_consts + ([] if final else [held["skip"]]),
            [held["enc_xhat"], held["enc_rstd"]] + tied,
            [("enc_gain", gain_kept)],
            early + [("late", late_shape)],
            cols,
            enc_flops,
            passed,
        )

    chain = [(enc_forward, level, level) for level in range(sections)]
    chain += [(dec_forward, level, last - level) for level in range(sections)]
    chain += [(dec_backward, level, last - level) for level in reversed(range(sections))]
    chain += [(enc_backward, level, level) for level in reversed(range(sections))]
    starts = [0]
    for before, after in zip(chain, chain[1:]):
        lag = LAG if before[0] in (dec_forward, dec_backward) else LAG_BESIDE
        starts.append(starts[-1] + (1 if before[2] == after[2] else min(lag, steps)))
    order = sorted(
        (starts[place] + step, step, place) for place in range(len(chain)) for step in range(steps)
    )

    def dec_weight_grad(bulks):
        dec_span = tap_span(dec_out_rows, channels, DEC_TAPS, parts)
        return pl.pallas_call(
            functools.partial(dec_weight_kernel, sizes, dec_span, dec_out_rows),
            in_specs=[VM] * parts,
            out_specs=VM,
            out_shape=jax.ShapeDtypeStruct((dec_out_rows + 16, channels), BF16),
            scratch_shapes=[pltpu.VMEM((dec_span * channels, channels), F32)],
            compiler_params=params(),
            cost_estimate=pl.CostEstimate(
                flops=2 * dec_span * channels * channels * parts * total_rows,
                bytes_accessed=0,
                transcendentals=0,
            ),
        )(*[in_vmem(value) for value in bulks])

    dec_out_rows = DEC_TAPS * channels // parts
    values = {(0, step): start for step in range(steps)}
    bulks, dec_grad, early_far = [], None, None
    for _, step, place in order:
        run, level, section = chain[place]
        tied, passed = [], None
        moving = None
        if run is enc_forward and level == last - 1 and step == 0:
            passed = came
        if run is dec_backward and level == 0 and step > 0:
            tied = [values[place + 1, step - 1, "done"]] if (place + 1, step - 1, "done") in values else []
        if run is enc_backward and step == 0 and bulks and level <= last - 3 and dec_grad is None:
            tied = [bulks[-1]]
            if len(bulks) < parts:
                moving = moves[len(bulks) - 1]
                passed = bulks[moving[0]]
            else:
                dec_grad = dec_weight_grad(bulks)
                tied = [dec_grad]
        if run is enc_backward and level == 0 and step == steps - 1 and early_far is not None:
            tied = tied + [early_far]
        y = run(level, step, values[place, step], tied, passed)
        values[place, step, "done"] = y
        if run is enc_forward and level == last - 1 and step == 0:
            came = held["passed"]
            dec_taps, dec_gain = pl.pallas_call(
                join_kernel,
                in_specs=[ANY] * 2,
                out_specs=[VM] * 2,
                out_shape=[pltpu.VMEM(dec_taps.shape, BF16), pltpu.VMEM((1, channels), F32)],
                scratch_shapes=[pltpu.VMEM((16, channels), BF16), pltpu.SemaphoreType.DMA((3,))],
                compiler_params=params(),
            )(came, swapped(came, 1))
            dec_consts.extend([dec_taps, dec_gain, dec_keep, spread_matrix])
        if moving is not None:
            bulks[moving[0]] = held["passed"]
            bulks.append(swapped(held["passed"], moving[1]))
        if run is dec_backward and level == 0 and step == steps - 1:
            bulks = [held["bulk"], swapped(held["bulk"], moves[0][1])]
        if run is enc_backward and level == 0 and step == steps // 2 - 1:
            early_far = swapped(held["early"], moves[0][1])
        if place + 1 < len(chain):
            target = chain[place + 1][2]
            values[place + 1, step] = y if target == section else send(y, section, target - section)
    while len(bulks) < parts:
        source, apart = moves[len(bulks) - 1]
        bulks.append(swapped(bulks[source], apart))
    if dec_grad is None:
        dec_grad = dec_weight_grad(bulks)
    earlies = [held["early"], early_far]
    for source, apart in moves[1:]:
        earlies.append(swapped(earlies[source], apart))
    lates = [held["late"]] + [swapped(held["late"], distance) for distance in distances[1:]]
    enc_out_rows = ENC_TAPS * channels // parts
    enc_span = tap_span(enc_out_rows, channels, ENC_TAPS, parts)
    width = channels // parts
    enc_weight_out, enc_gain_out, dec_weight_out, dec_gain_out = pl.pallas_call(
        functools.partial(enc_weight_kernel, sizes, enc_span, enc_out_rows, parts),
        in_specs=[VM] * (3 * parts + 1),
        out_specs=[VM] * 4,
        out_shape=[
            jax.ShapeDtypeStruct((enc_out_rows, channels), F32),
            jax.ShapeDtypeStruct((1, width), F32),
            jax.ShapeDtypeStruct((dec_out_rows, channels), F32),
            jax.ShapeDtypeStruct((1, width), F32),
        ],
        scratch_shapes=[pltpu.VMEM((enc_span * channels, channels), F32)],
        compiler_params=params(),
        cost_estimate=pl.CostEstimate(
            flops=2 * enc_span * channels * channels * parts * total_rows,
            bytes_accessed=0,
            transcendentals=0,
        ),
    )(*[in_vmem(value) for value in bulks + earlies + lates + [mirrored(dec_grad)]])
    return (enc_weight_out[None], enc_gain_out, dec_weight_out[None], dec_gain_out)


def solution(mesh):
    placed = (
        P("dp", None, None, None, None),
        P("dp"),
        P("dp"),
        P("dp", None, None, None, None),
        P("dp", None),
        P("section", None, None),
        P("section", None),
        P("section", None, None),
        P("section", None),
    )
    return jax.shard_map(
        body,
        mesh=mesh,
        in_specs=placed,
        out_specs=(
            P("section", "dp", None),
            P("section", "dp"),
            P("section", "dp", None),
            P("section", "dp"),
        ),
        check_vma=False,
    )
```

```python
import functools
import math

import jax
import jax.numpy as jnp
import numpy as np
from jax import lax
from jax.experimental import pallas as pl
from jax.experimental.pallas import tpu as pltpu
from jax.sharding import PartitionSpec as P

GROUPS = 32
ENC_TAPS = 9
DEC_TAPS = 3
KERNELS_OF_A_CHAIN = 32
PAIRS_APART = 3
COST_SHARE = 16
BF16 = jnp.bfloat16
F32 = jnp.float32
VMEM_LIMIT = 32 * 1024 * 1024


def noise_level(timesteps):
    phase_arg = (timesteps.astype(F32) / 1000.0 + 0.008) / 1.008
    return jnp.cos(phase_arg * (math.pi / 2.0)) ** 2


def group_means(sums, spread_matrix, count, splits):
    rest = sums
    pieces = []
    for _ in range(splits - 1):
        piece = rest.astype(BF16).astype(F32)
        pieces.append(piece)
        rest = rest - piece
    pieces.append(rest)
    number = sums.shape[0]
    parts = jnp.concatenate(pieces, axis=0).astype(BF16)
    spread = jnp.dot(parts, spread_matrix, preferred_element_type=F32)
    total = spread[:number]
    for place in range(1, splits):
        total = total + spread[place * number : (place + 1) * number]
    folded = total.reshape(number // 8, 8, sums.shape[1])
    return jnp.sum(folded, axis=1, keepdims=True) * (1.0 / count)


def eight_rows(values):
    return jnp.sum(values.reshape(-1, 8, values.shape[-1]), axis=0)


def sigmoid(z):
    return 0.5 * jnp.tanh(0.5 * z) + 0.5


def spatial_shift(frames, row_offset, col_offset, height, width):
    step = row_offset * width + col_offset
    length = height * width
    moved = pltpu.roll(frames, (-step) % length, axis=1) if step % length else frames
    if row_offset == 0 and col_offset == 0:
        return moved
    place = lax.broadcasted_iota(jnp.int32, (1, length, 1), 1)
    row = place // width + row_offset
    col = place % width + col_offset
    inside = (row >= 0) & (row < height) & (col >= 0) & (col < width)
    return jnp.where(inside, moved, 0.0)


def spatial_columns_into(cols_ref, values_ref, sizes, sign):
    each = sizes.height * sizes.width
    pair = 2 * each
    channels = sizes.channels

    def one_pair(index, carry):
        place = pl.ds(pl.multiple_of(index * pair, pair), pair)
        frames = values_ref[place].reshape(2, each, channels)
        for tap in range(ENC_TAPS):
            moved = spatial_shift(
                frames, sign * (tap // 3 - 1), sign * (tap % 3 - 1), sizes.height, sizes.width
            )
            cols_ref[tap // 3, place, (tap % 3) * channels : (tap % 3 + 1) * channels] = (
                moved.reshape(pair, channels).astype(BF16)
            )
        return carry

    lax.fori_loop(0, sizes.rows // pair, one_pair, 0)


def temporal_pieces(values, frames, sign):
    samples, length, channels = values.shape
    each = length // frames
    blank = jnp.zeros((samples, each, channels), F32)
    before = jnp.concatenate([blank, values[:, : length - each]], axis=1)
    after = jnp.concatenate([values[:, each:], blank], axis=1)
    ordered = (before, values, after) if sign > 0 else (after, values, before)
    return [piece.reshape(samples * length, channels).astype(BF16) for piece in ordered]


def dot_nt(left, right):
    return lax.dot_general(left, right, (((1,), (1,)), ((), ())), preferred_element_type=F32)


class Sizes:
    def __init__(self, noise_draw, sections):
        self.micro, self.frames, self.height, self.width, self.channels = noise_draw.shape
        self.length = self.frames * self.height * self.width
        self.per_step = max(1, self.micro * sections // KERNELS_OF_A_CHAIN)
        self.steps = self.micro // self.per_step
        self.rows = self.per_step * self.length
        self.count = self.length * (self.channels // GROUPS)
        self.total = self.micro * self.length

    def split(self, level, step):
        return level > 0 or step < self.steps // 2

    def sample(self, index):
        return slice(index * self.length, (index + 1) * self.length)


def norm_forward(sizes, values_ref, gain, spread_matrix, xhat_ref, rstd_ref):
    samples = range(sizes.per_step)
    sums = jnp.concatenate([eight_rows(values_ref[sizes.sample(s)]) for s in samples], axis=0)
    mean = group_means(sums, spread_matrix, sizes.count, 3)
    squares = []
    for s in samples:
        center = values_ref[sizes.sample(s)] - mean[s]
        values_ref[sizes.sample(s)] = center
        squares.append(eight_rows(center * center))
    spread = group_means(jnp.concatenate(squares, axis=0), spread_matrix, sizes.count, 3)
    rstd = lax.rsqrt(spread + 1e-05)
    for s in samples:
        normed = values_ref[sizes.sample(s)] * rstd[s]
        xhat_ref[sizes.sample(s)] = normed
        rstd_ref[s] = rstd[s]
        z = normed * gain
        values_ref[sizes.sample(s)] = z * sigmoid(z)


def residual(sizes, step, base_ref, keep_ref, branch_ref):
    out = []
    for s in range(sizes.per_step):
        index = step * sizes.per_step + s
        keep = keep_ref[index : index + 1]
        out.append(base_ref[sizes.sample(s)] + keep * branch_ref[sizes.sample(s)])
    return jnp.concatenate(out, axis=0)


def gate(sizes, step, keep_ref, values):
    out = []
    for s in range(sizes.per_step):
        index = step * sizes.per_step + s
        out.append(keep_ref[index : index + 1] * values[sizes.sample(s)])
    return jnp.concatenate(out, axis=0)


def started(source, target, sem):
    copy = pltpu.make_async_copy(source, target, sem)
    copy.start()
    return copy


def parts_of(sizes, step):
    return pl.ds(step * sizes.rows, sizes.rows), pl.ds(step * sizes.per_step, sizes.per_step)


def store_norms(sizes, step, xhat_ref, rstd_ref, half_ref, xhat_far, rstd_far, bulk_far, first_row, sems):
    part, samples = parts_of(sizes, step)
    place = pl.ds(first_row + step * sizes.rows, sizes.rows)
    return [
        started(half_ref, bulk_far.at[place], sems.at[0]),
        started(xhat_ref, xhat_far.at[part], sems.at[1]),
        started(rstd_ref, rstd_far.at[samples], sems.at[2]),
    ]


def enc_forward_kernel(sizes, level, step, final, x_ref, w_ref, gain_ref, keep_ref, spread_ref, *refs):
    outs = refs[:-7]
    y_ref = outs[-4] if final else outs[-5]
    xhat_far, rstd_far, bulk_far = outs[-3:]
    cols_ref, base_ref, values_ref, xhat_ref, rstd_ref, half_ref, sems = refs[-7:]

    @pl.when(lax.axis_index("section") == level)
    def _():
        part, _ = parts_of(sizes, step)
        x = (x_ref[part] if level == 0 else x_ref[...]).astype(F32)
        base_ref[...] = x
        values_ref[...] = x
        norm_forward(
            sizes, values_ref, gain_ref[...], spread_ref[...], xhat_ref, rstd_ref
        )
        half_ref[...] = values_ref[...].astype(BF16)
        copies = store_norms(
            sizes, step, xhat_ref, rstd_ref, half_ref, xhat_far, rstd_far, bulk_far, 0, sems
        )
        spatial_columns_into(cols_ref, values_ref, sizes, 1)

        def add_third(third, carry):
            part = jnp.dot(cols_ref[third], w_ref[third], preferred_element_type=F32)
            values_ref[...] = jnp.where(third == 0, part, values_ref[...] + part)
            return carry

        lax.fori_loop(0, 3, add_third, 0)
        out = residual(sizes, step, base_ref, keep_ref, values_ref).astype(BF16)
        y_ref[...] = out
        if not final:
            outs[-4][part] = out
        for copy in copies:
            copy.wait()


def dec_forward_kernel(
    sizes, home, step, first, scale, x_ref, w_ref, gain_ref, keep_ref, spread_ref, skip_ref, *refs
):
    base_ref, values_ref, xhat_ref, rstd_ref, half_ref, sems = refs[-6:]
    y_ref, xhat_far, rstd_far, bulk_far = refs[-10:-6]

    @pl.when(lax.axis_index("section") == home)
    def _():
        part, _ = parts_of(sizes, step)
        x = x_ref[...].astype(F32)
        base_ref[...] = x
        values_ref[...] = x + (x if first else skip_ref[part].astype(F32))
        norm_forward(
            sizes, values_ref, gain_ref[...], spread_ref[...], xhat_ref, rstd_ref
        )
        half_ref[...] = values_ref[...].astype(BF16)
        copies = store_norms(
            sizes, step, xhat_ref, rstd_ref, half_ref, xhat_far, rstd_far, bulk_far, sizes.total, sems
        )
        act = values_ref[...].reshape(sizes.per_step, sizes.length, sizes.channels)
        columns = jnp.concatenate(temporal_pieces(act, sizes.frames, 1), axis=1)
        values_ref[...] = jnp.dot(columns, w_ref[...], preferred_element_type=F32)
        out = residual(sizes, step, base_ref, keep_ref, values_ref).astype(BF16)
        if scale is not None:
            noise = refs[0][part].astype(F32)
            out = ((out.astype(F32) - noise) * scale).astype(BF16)
        y_ref[...] = out
        for copy in copies:
            copy.wait()


def norm_back(sizes, cot_ref, gain, spread_matrix, xhat_ref, rstd_ref):
    samples = range(sizes.per_step)
    sums, products = [], []
    gain_rows = 0.0
    for s in samples:
        normed = xhat_ref[sizes.sample(s)]
        z = normed * gain
        sig = sigmoid(z)
        dz = cot_ref[sizes.sample(s)] * (sig * (1.0 + z * (1.0 - sig)))
        gain_rows = gain_rows + eight_rows(dz * normed)
        dn = dz * gain
        cot_ref[sizes.sample(s)] = dn
        sums.append(eight_rows(dn))
        products.append(eight_rows(dn * normed))
    means = group_means(jnp.concatenate(sums + products, axis=0), spread_matrix, sizes.count, 2)
    for s in samples:
        normed = xhat_ref[sizes.sample(s)]
        cot_ref[sizes.sample(s)] = rstd_ref[s] * (
            cot_ref[sizes.sample(s)] - means[s] - normed * means[sizes.per_step + s]
        )
    return gain_rows


def add_gain(sizes, step, gain_acc_ref, gain_rows, cot_far, first_row, half_ref, sem):
    total = gain_rows if step == 0 else gain_acc_ref[...] + gain_rows
    gain_acc_ref[...] = total
    if step == sizes.steps - 1:
        row = jnp.sum(total, axis=0, keepdims=True)
        tail = jnp.concatenate([row, jnp.zeros((15, sizes.channels), F32)], axis=0)
        half_ref[:16] = tail.astype(BF16)
        started(half_ref.at[pl.ds(0, 16)], cot_far.at[pl.ds(first_row, 16)], sem).wait()


def enc_backward_kernel(
    sizes, level, step, last, x_ref, w_ref, gain_ref, keep_ref, spread_ref, *refs
):
    xhat_far, rstd_far = refs[:2] if last else refs[1:3]
    cols_ref, base_ref, values_ref, xhat_ref, rstd_ref, half_ref, sems = refs[-7:]
    outs = refs[-11:-7] if sizes.split(level, step) else refs[-10:-7]
    y_ref, gain_acc_ref = outs[:2]
    late = step >= sizes.steps // 2
    cot_far = outs[-1] if late else outs[2]
    first_row = (step - (sizes.steps // 2 if late else 0)) * sizes.rows

    @pl.when(lax.axis_index("section") == level)
    def _():
        part, samples = parts_of(sizes, step)
        loads = [
            started(xhat_far.at[part], xhat_ref, sems.at[1]),
            started(rstd_far.at[samples], rstd_ref, sems.at[2]),
        ]
        t = x_ref[...]
        if not last:
            t = (t.astype(F32) + refs[0][part].astype(F32)).astype(BF16)
        t = t.astype(F32)
        base_ref[...] = t
        gated = gate(sizes, step, keep_ref, t)
        values_ref[...] = gated
        half_ref[...] = gated.astype(BF16)
        store = started(half_ref, cot_far.at[pl.ds(first_row, sizes.rows)], sems.at[0])
        spatial_columns_into(cols_ref, values_ref, sizes, -1)

        def add_third(third, carry):
            part = jnp.zeros((sizes.rows, sizes.channels), F32)
            for tap in range(3):
                where = slice(tap * sizes.channels, (tap + 1) * sizes.channels)
                part = part + dot_nt(cols_ref[third, :, where], w_ref[third, where, :])
            values_ref[...] = jnp.where(third == 0, part, values_ref[...] + part)
            return carry

        lax.fori_loop(0, 3, add_third, 0)
        for copy in loads:
            copy.wait()
        gain_rows = norm_back(
            sizes, values_ref, gain_ref[...], spread_ref[...], xhat_ref, rstd_ref
        )
        y_ref[...] = (base_ref[...] + values_ref[...]).astype(BF16)
        store.wait()
        rows = (sizes.steps - sizes.steps // 2) * sizes.rows
        add_gain(sizes, step, gain_acc_ref, gain_rows, cot_far, rows, half_ref, sems.at[0])


def dec_backward_kernel(
    sizes, home, step, first, x_ref, w_ref, gain_ref, keep_ref, spread_ref, xhat_far, rstd_far, *refs
):
    base_ref, values_ref, xhat_ref, rstd_ref, half_ref, sems = refs[-6:]
    outs = refs[:-6]
    y_ref, gain_acc_ref = outs[-3:-1] if first else outs[-4:-2]
    bulk_far = outs[-1]

    @pl.when(lax.axis_index("section") == home)
    def _():
        part, samples = parts_of(sizes, step)
        copies = [
            started(xhat_far.at[part], xhat_ref, sems.at[1]),
            started(rstd_far.at[samples], rstd_ref, sems.at[2]),
        ]
        g = x_ref[...].astype(F32)
        base_ref[...] = g
        gated = gate(sizes, step, keep_ref, g)
        half_ref[...] = gated.astype(BF16)
        place = pl.ds(2 * sizes.total + step * sizes.rows, sizes.rows)
        store = started(half_ref, bulk_far.at[place], sems.at[0])
        pieces = temporal_pieces(
            gated.reshape(sizes.per_step, sizes.length, sizes.channels), sizes.frames, -1
        )
        back = jnp.zeros((sizes.rows, sizes.channels), F32)
        for tap in range(DEC_TAPS):
            where = slice(tap * sizes.channels, (tap + 1) * sizes.channels)
            back = back + dot_nt(pieces[tap], w_ref[where, :])
        values_ref[...] = back
        for copy in copies:
            copy.wait()
        gain_rows = norm_back(
            sizes, values_ref, gain_ref[...], spread_ref[...], xhat_ref, rstd_ref
        )
        grad = values_ref[...]
        out = (base_ref[...] + grad).astype(BF16)
        skip_cot = grad.astype(BF16)
        if first:
            y_ref[...] = (out.astype(F32) + skip_cot.astype(F32)).astype(BF16)
        else:
            y_ref[...] = out
            outs[-2][part] = skip_cot
        store.wait()
        add_gain(
            sizes, step, gain_acc_ref, gain_rows, bulk_far, 3 * sizes.total, half_ref, sems.at[0]
        )


def tap_span(rows_out, channels, taps, parts):
    span = 0
    for index in range(parts):
        start = index * rows_out
        span = max(span, -(-(start % channels + rows_out) // channels))
    return min(span, taps)


def tap_products(sizes, taps, span, rows_out, act, cot, wide_ref):
    me = lax.axis_index("dp")
    rows = act.shape[0]
    base = jnp.minimum(me * rows_out // sizes.channels, taps - span)
    each = sizes.height * sizes.width
    for tap in range(taps):

        @pl.when((tap >= base) & (tap < base + span))
        def _(tap=tap):
            if taps == ENC_TAPS:
                frames = act.reshape(rows // each, each, sizes.channels)
                moved = spatial_shift(frames, tap // 3 - 1, tap % 3 - 1, sizes.height, sizes.width)
                moved = moved.reshape(rows, sizes.channels).astype(BF16)
            else:
                values = act.reshape(rows // sizes.length, sizes.length, sizes.channels)
                moved = temporal_pieces(values, sizes.frames, 1)[tap]
            place = pl.multiple_of((tap - base) * sizes.channels, sizes.channels)
            wide_ref[pl.ds(place, sizes.channels)] = lax.dot_general(
                moved, cot, (((0,), (0,)), ((), ())), preferred_element_type=F32
            )

    offset = pl.multiple_of(me * rows_out - base * sizes.channels, 16)
    return wide_ref[pl.ds(offset, rows_out)]


def gain_sum(pieces):
    total = 0.0
    for piece in pieces:
        total = total + piece.astype(F32)
    return total


def dec_weight_kernel(sizes, span, rows_out, parts, *refs):
    bulk_refs, (out_ref, gain_ref, wide_ref) = refs[:parts], refs[parts:]
    total = sizes.total
    act = jnp.concatenate([ref[total : 2 * total] for ref in bulk_refs], axis=0).astype(F32)
    cot = jnp.concatenate([ref[2 * total : 3 * total] for ref in bulk_refs], axis=0)
    out_ref[...] = tap_products(sizes, DEC_TAPS, span, rows_out, act, cot, wide_ref)
    own_lanes(parts, gain_ref, gain_sum([ref[3 * total :] for ref in bulk_refs])[:1])


def own_lanes(parts, out_ref, row):
    width = row.shape[1] // parts
    for index in range(parts):

        @pl.when(lax.axis_index("dp") == index)
        def _(index=index):
            out_ref[...] = row[:, index * width : (index + 1) * width]


def enc_weight_kernel(sizes, span, rows_out, parts, *refs):
    bulk_refs, rest = refs[:parts], refs[parts:]
    early_refs, late_refs = rest[:parts], rest[parts : 2 * parts]
    out_ref, gain_ref, wide_ref = rest[2 * parts :]
    act = jnp.concatenate([ref[: sizes.total] for ref in bulk_refs], axis=0).astype(F32)
    pieces = []
    late_rows = late_refs[0].shape[0] - 16
    for early, late in zip(early_refs, late_refs):
        pieces.extend([early[...], late[:late_rows]])
    cot = jnp.concatenate(pieces, axis=0)
    own_lanes(parts, gain_ref, gain_sum([late[late_rows:] for late in late_refs])[:1])
    out_ref[...] = tap_products(sizes, ENC_TAPS, span, rows_out, act, cot, wide_ref)


def prologue_kernel(
    sizes,
    sections,
    ids_far,
    times_far,
    keep_far,
    pool_ref,
    noise_ref,
    enc_ref,
    dec_ref,
    enc_out,
    dec_out,
    spread_out,
    start_out,
    enc_keep_out,
    dec_keep_out,
    ids_ref,
    times_ref,
    keep_ref,
    sems,
):
    small = [
        started(ids_far, ids_ref, sems.at[2]),
        started(times_far, times_ref, sems.at[3]),
        started(keep_far, keep_ref, sems.at[4]),
    ]
    copies = [
        started(enc_ref, enc_out, sems.at[0]),
        started(dec_ref, dec_out, sems.at[1]),
    ]
    channels = sizes.channels
    per_group = channels // GROUPS
    left = lax.broadcasted_iota(jnp.int32, (channels, channels), 0) // per_group
    right = lax.broadcasted_iota(jnp.int32, (channels, channels), 1) // per_group
    spread_out[...] = jnp.where(left == right, 1.0, 0.0).astype(BF16)
    for copy in small:
        copy.wait()
    own = lax.axis_index("section")
    row = lax.broadcasted_iota(jnp.int32, (sizes.micro, channels), 0)
    times = jnp.zeros((sizes.micro, channels), F32)
    enc_keep = jnp.zeros((sizes.micro, channels), F32)
    dec_keep = jnp.zeros((sizes.micro, channels), F32)
    for index in range(sizes.micro):
        here = row == index
        times = jnp.where(here, times_ref[index].astype(F32), times)
        enc_keep = jnp.where(here, keep_ref[index, own].astype(F32), enc_keep)
        dec_keep = jnp.where(here, keep_ref[index, sections + own].astype(F32), dec_keep)
    enc_keep_out[...] = enc_keep
    dec_keep_out[...] = dec_keep
    level = noise_level(times)
    clean_part, noise_part = jnp.sqrt(level), jnp.sqrt(1.0 - level)
    for first in range(0, sizes.micro, 2):
        place = slice(first * sizes.length, (first + 2) * sizes.length)
        noise = noise_ref[place].astype(F32)
        mixed = []
        for index in (first, first + 1):
            clean = pool_ref[ids_ref[index]].astype(F32)
            own_noise = noise[sizes.sample(index - first)]
            mixed.append(
                clean_part[index : index + 1] * clean + noise_part[index : index + 1] * own_noise
            )
        start_out[place] = jnp.concatenate(mixed, axis=0).astype(BF16)
    for copy in copies:
        copy.wait()


def passing(kernel, scratch_count):
    def run(*refs):
        cut = len(refs) - scratch_count - 1
        kernel(*refs[:cut], *refs[cut + 1 :])

    return run


VM = pl.BlockSpec(memory_space=pltpu.VMEM)
ANY = pl.BlockSpec(memory_space=pl.ANY)


def params():
    return pltpu.CompilerParams(vmem_limit_bytes=VMEM_LIMIT)


def in_vmem(value):
    return pltpu.with_memory_space_constraint(value, pltpu.VMEM)


def staged_call(kernel, near, distant, plain_outs, kept, far, state, passed, scratch, flops):
    state = list(state) if state is not None else [None] * (len(kept) + len(far))
    inputs = [in_vmem(value) for value in near] + list(distant)
    in_specs = [VM] * len(near) + [ANY] * len(distant)
    aliases = {}
    for place, value in enumerate(state):
        if value is None:
            continue
        aliases[len(inputs)] = len(plain_outs) + place
        close = place < len(kept)
        inputs.append(in_vmem(value) if close else value)
        in_specs.append(VM if close else ANY)
    out_specs = [VM] * (len(plain_outs) + len(kept)) + [ANY] * len(far)
    out_shape = [pltpu.VMEM(s, d) for s, d in list(plain_outs) + list(kept)]
    out_shape += [jax.ShapeDtypeStruct(s, d) for s, d in far]
    if passed is not None:
        value, close = passed
        kernel = passing(kernel, len(scratch))
        aliases[len(inputs)] = len(out_specs)
        inputs.append(in_vmem(value) if close else value)
        in_specs.append(VM if close else ANY)
        out_specs.append(VM if close else ANY)
        kind = pltpu.VMEM if close else jax.ShapeDtypeStruct
        out_shape.append(kind(value.shape, value.dtype))
    outs = pl.pallas_call(
        kernel,
        in_specs=in_specs,
        out_specs=out_specs,
        out_shape=out_shape,
        scratch_shapes=scratch,
        input_output_aliases=aliases,
        compiler_params=params(),
        cost_estimate=pl.CostEstimate(flops=flops // COST_SHARE, bytes_accessed=0, transcendentals=0),
    )(*inputs)
    return list(outs[: len(plain_outs)]), list(outs[len(plain_outs) :])


def body(
    clip_pool,
    sample_ids,
    timesteps,
    noise_draw,
    keep_lists,
    enc_weight,
    enc_gain,
    dec_weight,
    dec_gain,
):
    sections = lax.axis_size("section")
    parts = lax.axis_size("dp")
    sizes = Sizes(noise_draw, sections)
    channels, rows, steps, total_rows = sizes.channels, sizes.rows, sizes.steps, sizes.total
    scale = 1.0 / math.sqrt(sizes.micro * parts * sizes.length)
    last = sections - 1

    def send(value, source, by):
        pairs = [
            (other, (other + by) % sections)
            for other in range(source % PAIRS_APART, sections, PAIRS_APART)
        ]
        return lax.ppermute(value, "section", pairs)

    def mirrored(value):
        return lax.ppermute(value, "section", [(i, last - i) for i in range(sections)])

    def swapped(value, apart):
        return lax.ppermute(value, "dp", [(i, i ^ apart) for i in range(parts)])

    moves = []
    distances = [0]
    apart = parts // 2
    while apart:
        moves += [(place, apart) for place in range(len(distances))]
        distances += [distance ^ apart for distance in distances]
        apart //= 2

    clips = clip_pool.reshape(clip_pool.shape[0], sizes.length, channels)
    noise = noise_draw.reshape(total_rows, channels)
    enc_taps = enc_weight.reshape(3, 3 * channels, channels)
    dec_taps = dec_weight.reshape(DEC_TAPS * channels, channels)
    enc_taps, dec_taps, spread_matrix, start, enc_keep, dec_keep = pl.pallas_call(
        functools.partial(prologue_kernel, sizes, sections),
        in_specs=[ANY] * 3 + [VM] * 2 + [pl.BlockSpec(memory_space=pltpu.HBM)] * 2,
        out_specs=[VM] * 6,
        out_shape=[
            pltpu.VMEM(enc_taps.shape, BF16),
            pltpu.VMEM(dec_taps.shape, BF16),
            pltpu.VMEM((channels, channels), BF16),
            pltpu.VMEM(noise.shape, BF16),
            pltpu.VMEM((sizes.micro, channels), F32),
            pltpu.VMEM((sizes.micro, channels), F32),
        ],
        scratch_shapes=[
            pltpu.SMEM(sample_ids.shape, jnp.int32),
            pltpu.SMEM(timesteps.shape, jnp.int32),
            pltpu.SMEM(keep_lists.shape, jnp.int32),
            pltpu.SemaphoreType.DMA((5,)),
        ],
        compiler_params=params(),
    )(
        sample_ids,
        timesteps,
        keep_lists,
        clips,
        noise,
        pltpu.with_memory_space_constraint(enc_taps, pltpu.HBM),
        pltpu.with_memory_space_constraint(dec_taps, pltpu.HBM),
    )
    row_shape = ((rows, channels), BF16)
    all_rows = ((total_rows, channels), BF16)
    bulk_shape = ((3 * total_rows + 16, channels), BF16)
    norm_far = [((total_rows, channels), F32), ((sizes.micro, 1, channels), F32)]
    gain_kept = ((8, channels), F32)
    early_rows = (steps // 2) * rows
    early_shape = ((early_rows, channels), BF16)
    late_shape = ((total_rows - early_rows + 16, channels), BF16)
    work = [
        pltpu.VMEM((rows, channels), F32),
        pltpu.VMEM((rows, channels), F32),
        pltpu.VMEM((rows, channels), F32),
        pltpu.VMEM((sizes.per_step, 1, channels), F32),
        pltpu.VMEM((rows, channels), BF16),
        pltpu.SemaphoreType.DMA((3,)),
    ]
    cols = [pltpu.VMEM((3, rows, 3 * channels), BF16)] + work
    enc_flops = 2 * rows * ENC_TAPS * channels * channels
    dec_flops = 2 * rows * DEC_TAPS * channels * channels
    enc_consts = [enc_taps, enc_gain, enc_keep, spread_matrix]
    dec_consts = [dec_taps, dec_gain, dec_keep, spread_matrix]
    held = {}

    def stage(kernel, near, distant, kept, far, passed, scratch, flops):
        names = [name for name, _ in kept + far]
        (y,), state = staged_call(
            kernel,
            near,
            distant,
            [row_shape],
            [shape for _, shape in kept],
            [shape for _, shape in far],
            [held.get(name) for name in names],
            passed,
            scratch,
            flops,
        )
        held.update(zip(names + ["passed"], state))
        return y

    def enc_forward(level, step, x, tied, passed):
        return stage(
            functools.partial(enc_forward_kernel, sizes, level, step, level == last),
            [x] + enc_consts,
            tied,
            [("out", all_rows)] if level < last else [],
            [("enc_xhat", norm_far[0]), ("enc_rstd", norm_far[1]), ("bulk", bulk_shape)],
            passed,
            cols,
            enc_flops,
        )

    def dec_forward(level, step, x, tied, passed):
        final = level == last
        return stage(
            functools.partial(
                dec_forward_kernel, sizes, level, step, level == 0, scale if final else None
            ),
            [x] + dec_consts + [x if level == 0 else held["came"]] + ([noise] if final else []),
            tied,
            [],
            [("dec_xhat", norm_far[0]), ("dec_rstd", norm_far[1]), ("bulk", bulk_shape)],
            passed,
            work,
            dec_flops,
        )

    def dec_backward(level, step, g, tied, passed):
        return stage(
            functools.partial(dec_backward_kernel, sizes, level, step, level == 0),
            [g] + dec_consts,
            [held["dec_xhat"], held["dec_rstd"]] + tied,
            [("dec_gain", gain_kept)] + ([("skip", all_rows)] if level > 0 else []),
            [("bulk", bulk_shape)],
            passed,
            work,
            dec_flops,
        )

    def enc_backward(level, step, t, tied, passed):
        final = level == last
        early = [("early", early_shape)] if sizes.split(level, step) else []
        return stage(
            functools.partial(enc_backward_kernel, sizes, level, step, final),
            [t] + enc_consts + ([] if final else [held["came back"]]),
            [held["enc_xhat"], held["enc_rstd"]] + tied,
            [("enc_gain", gain_kept)],
            early + [("late", late_shape)],
            passed,
            cols,
            enc_flops,
        )

    chain = [(enc_forward, level, level) for level in range(sections)]
    chain += [(dec_forward, level, level) for level in range(sections)]
    chain += [(dec_backward, level, level) for level in reversed(range(sections))]
    chain += [(enc_backward, level, level) for level in reversed(range(sections))]
    starts = [0]
    for before, after in zip(chain, chain[1:]):
        starts.append(starts[-1] + (1 if before[2] == after[2] else steps))
    order = sorted(
        (starts[place] + step, step, place) for place in range(len(chain)) for step in range(steps)
    )

    dec_out_rows = DEC_TAPS * channels // parts
    dec_span = tap_span(dec_out_rows, channels, DEC_TAPS, parts)
    width = channels // parts
    values = {(0, step): start for step in range(steps)}
    early_far = None
    for _, step, place in order:
        run, level, section = chain[place]
        tied, passed = [], None
        turning = (run is enc_forward and level == last - 1) or (run is dec_backward and level == 1)
        if run is dec_forward and level == 0 and step == 0:
            tied = [held["came"]]
        if run is enc_backward and level == last and step == 0:
            tied = [held["came back"]]
        if run is enc_backward and level == 0 and step == steps - 1:
            passed = (held["bulk"], False)
        if run is enc_backward and level == 0 and step == steps - 1 and early_far is not None:
            tied = [early_far]
        y = run(level, step, values[place, step], tied, passed)
        if turning and step == steps - 1:
            if run is enc_forward:
                held["came"] = mirrored(held["out"])
            else:
                held["came back"] = mirrored(held["skip"])
        if run is enc_backward and level == 0 and step == steps - 1:
            bulks = [held["passed"]]
        if run is enc_backward and level == 0 and step == steps // 2 - 1:
            early_far = swapped(held["early"], moves[0][1])
        if place + 1 < len(chain):
            target = chain[place + 1][2]
            by = 1 if run in (enc_forward, dec_forward) else -1
            values[place + 1, step] = y if target == section else send(y, section, by)
    for source, apart in moves:
        bulks.append(swapped(bulks[source], apart))
    dec_weight_out, dec_gain_out = pl.pallas_call(
        functools.partial(dec_weight_kernel, sizes, dec_span, dec_out_rows, parts),
        in_specs=[VM] * parts,
        out_specs=[VM] * 2,
        out_shape=[
            jax.ShapeDtypeStruct((dec_out_rows, channels), F32),
            jax.ShapeDtypeStruct((1, width), F32),
        ],
        scratch_shapes=[pltpu.VMEM((dec_span * channels, channels), F32)],
        compiler_params=params(),
        cost_estimate=pl.CostEstimate(
            flops=2 * dec_span * channels * channels * parts * total_rows,
            bytes_accessed=0,
            transcendentals=0,
        ),
    )(*[in_vmem(value) for value in bulks])
    earlies = [held["early"], early_far]
    for source, apart in moves[1:]:
        earlies.append(swapped(earlies[source], apart))
    lates = [held["late"]] + [swapped(held["late"], distance) for distance in distances[1:]]
    enc_out_rows = ENC_TAPS * channels // parts
    enc_span = tap_span(enc_out_rows, channels, ENC_TAPS, parts)
    enc_weight_out, enc_gain_out = pl.pallas_call(
        functools.partial(enc_weight_kernel, sizes, enc_span, enc_out_rows, parts),
        in_specs=[VM] * (3 * parts),
        out_specs=[VM] * 2,
        out_shape=[
            jax.ShapeDtypeStruct((enc_out_rows, channels), F32),
            jax.ShapeDtypeStruct((1, width), F32),
        ],
        scratch_shapes=[pltpu.VMEM((enc_span * channels, channels), F32)],
        compiler_params=params(),
        cost_estimate=pl.CostEstimate(
            flops=2 * enc_span * channels * channels * parts * total_rows,
            bytes_accessed=0,
            transcendentals=0,
        ),
    )(*[in_vmem(value) for value in bulks + earlies + lates])
    return (enc_weight_out[None], enc_gain_out, dec_weight_out[None], dec_gain_out)


def solution(mesh):
    placed = (
        P("dp", None, None, None, None),
        P("dp"),
        P("dp"),
        P("dp", None, None, None, None),
        P("dp", None),
        P("section", None, None),
        P("section", None),
        P("section", None, None),
        P("section", None),
    )
    return jax.shard_map(
        body,
        mesh=mesh,
        in_specs=placed,
        out_specs=(
            P("section", "dp", None),
            P("section", "dp"),
            P("section", "dp", None),
            P("section", "dp"),
        ),
        check_vma=False,
    )
```

```python
import functools
import math

import jax
import jax.numpy as jnp
import numpy as np
from jax import lax
from jax.experimental import pallas as pl
from jax.experimental.pallas import tpu as pltpu
from jax.sharding import PartitionSpec as P

GROUPS = 32
ENC_TAPS = 9
DEC_TAPS = 3
KERNELS_OF_A_CHAIN = 32
PAIRS_APART = 3
COST_SHARE = 16
BF16 = jnp.bfloat16
F32 = jnp.float32
VMEM_LIMIT = 32 * 1024 * 1024


def noise_level(timesteps):
    phase_arg = (timesteps.astype(F32) / 1000.0 + 0.008) / 1.008
    return jnp.cos(phase_arg * (math.pi / 2.0)) ** 2


def group_means(sums, spread_matrix, count, splits):
    rest = sums
    pieces = []
    for _ in range(splits - 1):
        piece = rest.astype(BF16).astype(F32)
        pieces.append(piece)
        rest = rest - piece
    pieces.append(rest)
    number = sums.shape[0]
    parts = jnp.concatenate(pieces, axis=0).astype(BF16)
    spread = jnp.dot(parts, spread_matrix, preferred_element_type=F32)
    total = spread[:number]
    for place in range(1, splits):
        total = total + spread[place * number : (place + 1) * number]
    folded = total.reshape(number // 8, 8, sums.shape[1])
    return jnp.sum(folded, axis=1, keepdims=True) * (1.0 / count)


def eight_rows(values):
    return jnp.sum(values.reshape(-1, 8, values.shape[-1]), axis=0)


def sigmoid(z):
    return 0.5 * jnp.tanh(0.5 * z) + 0.5


def spatial_shift(frames, row_offset, col_offset, height, width):
    step = row_offset * width + col_offset
    length = height * width
    moved = pltpu.roll(frames, (-step) % length, axis=1) if step % length else frames
    if row_offset == 0 and col_offset == 0:
        return moved
    place = lax.broadcasted_iota(jnp.int32, (1, length, 1), 1)
    row = place // width + row_offset
    col = place % width + col_offset
    inside = (row >= 0) & (row < height) & (col >= 0) & (col < width)
    return jnp.where(inside, moved, 0.0)


def spatial_columns_into(cols_ref, values_ref, sizes, sign):
    each = sizes.height * sizes.width
    pair = 2 * each
    channels = sizes.channels

    def one_pair(index, carry):
        place = pl.ds(pl.multiple_of(index * pair, pair), pair)
        frames = values_ref[place].reshape(2, each, channels)
        for tap in range(ENC_TAPS):
            moved = spatial_shift(
                frames, sign * (tap // 3 - 1), sign * (tap % 3 - 1), sizes.height, sizes.width
            )
            cols_ref[tap // 3, place, (tap % 3) * channels : (tap % 3 + 1) * channels] = (
                moved.reshape(pair, channels).astype(BF16)
            )
        return carry

    lax.fori_loop(0, sizes.rows // pair, one_pair, 0)


def temporal_pieces(values, frames, sign):
    samples, length, channels = values.shape
    each = length // frames
    blank = jnp.zeros((samples, each, channels), F32)
    before = jnp.concatenate([blank, values[:, : length - each]], axis=1)
    after = jnp.concatenate([values[:, each:], blank], axis=1)
    ordered = (before, values, after) if sign > 0 else (after, values, before)
    return [piece.reshape(samples * length, channels).astype(BF16) for piece in ordered]


def dot_nt(left, right):
    return lax.dot_general(left, right, (((1,), (1,)), ((), ())), preferred_element_type=F32)


class Sizes:
    def __init__(self, noise_draw, sections):
        self.micro, self.frames, self.height, self.width, self.channels = noise_draw.shape
        self.length = self.frames * self.height * self.width
        self.per_step = max(1, self.micro * sections // KERNELS_OF_A_CHAIN)
        self.steps = self.micro // self.per_step
        self.rows = self.per_step * self.length
        self.count = self.length * (self.channels // GROUPS)
        self.total = self.micro * self.length

    def split(self, level, step):
        return level > 0 or step < self.steps // 2

    def sample(self, index):
        return slice(index * self.length, (index + 1) * self.length)


def norm_forward(sizes, values_ref, gain, spread_matrix, xhat_ref, rstd_ref):
    samples = range(sizes.per_step)
    sums = jnp.concatenate([eight_rows(values_ref[sizes.sample(s)]) for s in samples], axis=0)
    mean = group_means(sums, spread_matrix, sizes.count, 3)
    squares = []
    for s in samples:
        center = values_ref[sizes.sample(s)] - mean[s]
        values_ref[sizes.sample(s)] = center
        squares.append(eight_rows(center * center))
    spread = group_means(jnp.concatenate(squares, axis=0), spread_matrix, sizes.count, 3)
    rstd = lax.rsqrt(spread + 1e-05)
    for s in samples:
        normed = values_ref[sizes.sample(s)] * rstd[s]
        xhat_ref[sizes.sample(s)] = normed
        rstd_ref[s] = rstd[s]
        z = normed * gain
        values_ref[sizes.sample(s)] = z * sigmoid(z)


def residual(sizes, step, base_ref, keep_ref, branch_ref):
    out = []
    for s in range(sizes.per_step):
        index = step * sizes.per_step + s
        keep = keep_ref[index : index + 1]
        out.append(base_ref[sizes.sample(s)] + keep * branch_ref[sizes.sample(s)])
    return jnp.concatenate(out, axis=0)


def gate(sizes, step, keep_ref, values):
    out = []
    for s in range(sizes.per_step):
        index = step * sizes.per_step + s
        out.append(keep_ref[index : index + 1] * values[sizes.sample(s)])
    return jnp.concatenate(out, axis=0)


def started(source, target, sem):
    copy = pltpu.make_async_copy(source, target, sem)
    copy.start()
    return copy


def parts_of(sizes, step):
    return pl.ds(step * sizes.rows, sizes.rows), pl.ds(step * sizes.per_step, sizes.per_step)


def store_norms(sizes, step, xhat_ref, rstd_ref, half_ref, xhat_far, rstd_far, bulk_far, first_row, sems):
    part, samples = parts_of(sizes, step)
    place = pl.ds(first_row + step * sizes.rows, sizes.rows)
    return [
        started(half_ref, bulk_far.at[place], sems.at[0]),
        started(xhat_ref, xhat_far.at[part], sems.at[1]),
        started(rstd_ref, rstd_far.at[samples], sems.at[2]),
    ]


def enc_forward_kernel(sizes, level, step, final, x_ref, w_ref, gain_ref, keep_ref, spread_ref, *refs):
    outs = refs[:-7]
    y_ref = outs[-4] if final else outs[-5]
    xhat_far, rstd_far, bulk_far = outs[-3:]
    cols_ref, base_ref, values_ref, xhat_ref, rstd_ref, half_ref, sems = refs[-7:]

    @pl.when(lax.axis_index("section") == level)
    def _():
        part, _ = parts_of(sizes, step)
        x = (x_ref[part] if level == 0 else x_ref[...]).astype(F32)
        base_ref[...] = x
        values_ref[...] = x
        norm_forward(
            sizes, values_ref, gain_ref[...], spread_ref[...], xhat_ref, rstd_ref
        )
        half_ref[...] = values_ref[...].astype(BF16)
        copies = store_norms(
            sizes, step, xhat_ref, rstd_ref, half_ref, xhat_far, rstd_far, bulk_far, 0, sems
        )
        spatial_columns_into(cols_ref, values_ref, sizes, 1)

        def add_third(third, carry):
            part = jnp.dot(cols_ref[third], w_ref[third], preferred_element_type=F32)
            values_ref[...] = jnp.where(third == 0, part, values_ref[...] + part)
            return carry

        lax.fori_loop(0, 3, add_third, 0)
        out = residual(sizes, step, base_ref, keep_ref, values_ref).astype(BF16)
        y_ref[...] = out
        if not final:
            outs[-4][part] = out
        for copy in copies:
            copy.wait()


def dec_forward_kernel(
    sizes, home, step, first, scale, x_ref, w_ref, gain_ref, keep_ref, spread_ref, skip_ref, *refs
):
    base_ref, values_ref, xhat_ref, rstd_ref, half_ref, sems = refs[-6:]
    y_ref, xhat_far, rstd_far, bulk_far = refs[-10:-6]

    @pl.when(lax.axis_index("section") == home)
    def _():
        part, _ = parts_of(sizes, step)
        x = x_ref[...].astype(F32)
        base_ref[...] = x
        values_ref[...] = x + (x if first else skip_ref[part].astype(F32))
        norm_forward(
            sizes, values_ref, gain_ref[...], spread_ref[...], xhat_ref, rstd_ref
        )
        half_ref[...] = values_ref[...].astype(BF16)
        copies = store_norms(
            sizes, step, xhat_ref, rstd_ref, half_ref, xhat_far, rstd_far, bulk_far, sizes.total, sems
        )
        act = values_ref[...].reshape(sizes.per_step, sizes.length, sizes.channels)
        columns = jnp.concatenate(temporal_pieces(act, sizes.frames, 1), axis=1)
        values_ref[...] = jnp.dot(columns, w_ref[...], preferred_element_type=F32)
        out = residual(sizes, step, base_ref, keep_ref, values_ref).astype(BF16)
        if scale is not None:
            noise = refs[0][part].astype(F32)
            out = ((out.astype(F32) - noise) * scale).astype(BF16)
        y_ref[...] = out
        for copy in copies:
            copy.wait()


def norm_back(sizes, cot_ref, gain, spread_matrix, xhat_ref, rstd_ref):
    samples = range(sizes.per_step)
    sums, products = [], []
    gain_rows = 0.0
    for s in samples:
        normed = xhat_ref[sizes.sample(s)]
        z = normed * gain
        sig = sigmoid(z)
        dz = cot_ref[sizes.sample(s)] * (sig * (1.0 + z * (1.0 - sig)))
        gain_rows = gain_rows + eight_rows(dz * normed)
        dn = dz * gain
        cot_ref[sizes.sample(s)] = dn
        sums.append(eight_rows(dn))
        products.append(eight_rows(dn * normed))
    means = group_means(jnp.concatenate(sums + products, axis=0), spread_matrix, sizes.count, 2)
    for s in samples:
        normed = xhat_ref[sizes.sample(s)]
        cot_ref[sizes.sample(s)] = rstd_ref[s] * (
            cot_ref[sizes.sample(s)] - means[s] - normed * means[sizes.per_step + s]
        )
    return gain_rows


def add_gain(sizes, step, gain_acc_ref, gain_rows, cot_far, first_row, half_ref, sem):
    total = gain_rows if step == 0 else gain_acc_ref[...] + gain_rows
    gain_acc_ref[...] = total
    if step == sizes.steps - 1:
        row = jnp.sum(total, axis=0, keepdims=True)
        tail = jnp.concatenate([row, jnp.zeros((15, sizes.channels), F32)], axis=0)
        half_ref[:16] = tail.astype(BF16)
        started(half_ref.at[pl.ds(0, 16)], cot_far.at[pl.ds(first_row, 16)], sem).wait()


def enc_backward_kernel(
    sizes, level, step, last, x_ref, w_ref, gain_ref, keep_ref, spread_ref, *refs
):
    xhat_far, rstd_far = refs[:2] if last else refs[1:3]
    cols_ref, base_ref, values_ref, xhat_ref, rstd_ref, half_ref, sems = refs[-7:]
    outs = refs[-11:-7] if sizes.split(level, step) else refs[-10:-7]
    y_ref, gain_acc_ref = outs[:2]
    late = step >= sizes.steps // 2
    cot_far = outs[-1] if late else outs[2]
    first_row = (step - (sizes.steps // 2 if late else 0)) * sizes.rows

    @pl.when(lax.axis_index("section") == level)
    def _():
        part, samples = parts_of(sizes, step)
        loads = [
            started(xhat_far.at[part], xhat_ref, sems.at[1]),
            started(rstd_far.at[samples], rstd_ref, sems.at[2]),
        ]
        t = x_ref[...]
        if not last:
            t = (t.astype(F32) + refs[0][part].astype(F32)).astype(BF16)
        t = t.astype(F32)
        base_ref[...] = t
        gated = gate(sizes, step, keep_ref, t)
        values_ref[...] = gated
        half_ref[...] = gated.astype(BF16)
        store = started(half_ref, cot_far.at[pl.ds(first_row, sizes.rows)], sems.at[0])
        spatial_columns_into(cols_ref, values_ref, sizes, -1)

        def add_third(third, carry):
            part = jnp.zeros((sizes.rows, sizes.channels), F32)
            for tap in range(3):
                where = slice(tap * sizes.channels, (tap + 1) * sizes.channels)
                part = part + dot_nt(cols_ref[third, :, where], w_ref[third, where, :])
            values_ref[...] = jnp.where(third == 0, part, values_ref[...] + part)
            return carry

        lax.fori_loop(0, 3, add_third, 0)
        for copy in loads:
            copy.wait()
        gain_rows = norm_back(
            sizes, values_ref, gain_ref[...], spread_ref[...], xhat_ref, rstd_ref
        )
        y_ref[...] = (base_ref[...] + values_ref[...]).astype(BF16)
        store.wait()
        rows = (sizes.steps - sizes.steps // 2) * sizes.rows
        add_gain(sizes, step, gain_acc_ref, gain_rows, cot_far, rows, half_ref, sems.at[0])


def dec_backward_kernel(
    sizes, home, step, first, x_ref, w_ref, gain_ref, keep_ref, spread_ref, xhat_far, rstd_far, *refs
):
    base_ref, values_ref, xhat_ref, rstd_ref, half_ref, sems = refs[-6:]
    outs = refs[:-6]
    y_ref, gain_acc_ref = outs[-3:-1] if first else outs[-4:-2]
    bulk_far = outs[-1]

    @pl.when(lax.axis_index("section") == home)
    def _():
        part, samples = parts_of(sizes, step)
        copies = [
            started(xhat_far.at[part], xhat_ref, sems.at[1]),
            started(rstd_far.at[samples], rstd_ref, sems.at[2]),
        ]
        g = x_ref[...].astype(F32)
        base_ref[...] = g
        gated = gate(sizes, step, keep_ref, g)
        half_ref[...] = gated.astype(BF16)
        place = pl.ds(2 * sizes.total + step * sizes.rows, sizes.rows)
        store = started(half_ref, bulk_far.at[place], sems.at[0])
        pieces = temporal_pieces(
            gated.reshape(sizes.per_step, sizes.length, sizes.channels), sizes.frames, -1
        )
        back = jnp.zeros((sizes.rows, sizes.channels), F32)
        for tap in range(DEC_TAPS):
            where = slice(tap * sizes.channels, (tap + 1) * sizes.channels)
            back = back + dot_nt(pieces[tap], w_ref[where, :])
        values_ref[...] = back
        for copy in copies:
            copy.wait()
        gain_rows = norm_back(
            sizes, values_ref, gain_ref[...], spread_ref[...], xhat_ref, rstd_ref
        )
        grad = values_ref[...]
        out = (base_ref[...] + grad).astype(BF16)
        skip_cot = grad.astype(BF16)
        if first:
            y_ref[...] = (out.astype(F32) + skip_cot.astype(F32)).astype(BF16)
        else:
            y_ref[...] = out
            outs[-2][part] = skip_cot
        store.wait()
        add_gain(
            sizes, step, gain_acc_ref, gain_rows, bulk_far, 3 * sizes.total, half_ref, sems.at[0]
        )


def tap_span(rows_out, channels, taps, parts):
    span = 0
    for index in range(parts):
        start = index * rows_out
        span = max(span, -(-(start % channels + rows_out) // channels))
    return min(span, taps)


def tap_products(sizes, taps, span, rows_out, act, cot, wide_ref):
    me = lax.axis_index("dp")
    rows = act.shape[0]
    base = jnp.minimum(me * rows_out // sizes.channels, taps - span)
    each = sizes.height * sizes.width
    for tap in range(taps):

        @pl.when((tap >= base) & (tap < base + span))
        def _(tap=tap):
            if taps == ENC_TAPS:
                frames = act.reshape(rows // each, each, sizes.channels)
                moved = spatial_shift(frames, tap // 3 - 1, tap % 3 - 1, sizes.height, sizes.width)
                moved = moved.reshape(rows, sizes.channels).astype(BF16)
            else:
                values = act.reshape(rows // sizes.length, sizes.length, sizes.channels)
                moved = temporal_pieces(values, sizes.frames, 1)[tap]
            place = pl.multiple_of((tap - base) * sizes.channels, sizes.channels)
            wide_ref[pl.ds(place, sizes.channels)] = lax.dot_general(
                moved, cot, (((0,), (0,)), ((), ())), preferred_element_type=F32
            )

    offset = pl.multiple_of(me * rows_out - base * sizes.channels, 16)
    return wide_ref[pl.ds(offset, rows_out)]


def gain_sum(pieces):
    total = 0.0
    for piece in pieces:
        total = total + piece.astype(F32)
    return total


def dec_weight_kernel(sizes, span, rows_out, parts, *refs):
    bulk_refs, (out_ref, gain_ref, wide_ref) = refs[:parts], refs[parts:]
    total = sizes.total
    act = jnp.concatenate([ref[total : 2 * total] for ref in bulk_refs], axis=0).astype(F32)
    cot = jnp.concatenate([ref[2 * total : 3 * total] for ref in bulk_refs], axis=0)
    out_ref[...] = tap_products(sizes, DEC_TAPS, span, rows_out, act, cot, wide_ref)
    own_lanes(parts, gain_ref, gain_sum([ref[3 * total :] for ref in bulk_refs])[:1])


def own_lanes(parts, out_ref, row):
    width = row.shape[1] // parts
    for index in range(parts):

        @pl.when(lax.axis_index("dp") == index)
        def _(index=index):
            out_ref[...] = row[:, index * width : (index + 1) * width]


def enc_weight_kernel(sizes, span, rows_out, parts, *refs):
    bulk_refs, rest = refs[:parts], refs[parts:]
    early_refs, late_refs = rest[:parts], rest[parts : 2 * parts]
    out_ref, gain_ref, wide_ref = rest[2 * parts :]
    act = jnp.concatenate([ref[: sizes.total] for ref in bulk_refs], axis=0).astype(F32)
    pieces = []
    late_rows = late_refs[0].shape[0] - 16
    for early, late in zip(early_refs, late_refs):
        pieces.extend([early[...], late[:late_rows]])
    cot = jnp.concatenate(pieces, axis=0)
    own_lanes(parts, gain_ref, gain_sum([late[late_rows:] for late in late_refs])[:1])
    out_ref[...] = tap_products(sizes, ENC_TAPS, span, rows_out, act, cot, wide_ref)


def prologue_kernel(
    sizes,
    sections,
    ids_far,
    times_far,
    keep_far,
    pool_ref,
    noise_ref,
    enc_ref,
    dec_ref,
    enc_out,
    dec_out,
    spread_out,
    start_out,
    enc_keep_out,
    dec_keep_out,
    ids_ref,
    times_ref,
    keep_ref,
    sems,
):
    small = [
        started(ids_far, ids_ref, sems.at[2]),
        started(times_far, times_ref, sems.at[3]),
        started(keep_far, keep_ref, sems.at[4]),
    ]
    copies = [
        started(enc_ref, enc_out, sems.at[0]),
        started(dec_ref, dec_out, sems.at[1]),
    ]
    channels = sizes.channels
    per_group = channels // GROUPS
    left = lax.broadcasted_iota(jnp.int32, (channels, channels), 0) // per_group
    right = lax.broadcasted_iota(jnp.int32, (channels, channels), 1) // per_group
    spread_out[...] = jnp.where(left == right, 1.0, 0.0).astype(BF16)
    for copy in small:
        copy.wait()
    own = lax.axis_index("section")
    row = lax.broadcasted_iota(jnp.int32, (sizes.micro, channels), 0)
    times = jnp.zeros((sizes.micro, channels), F32)
    enc_keep = jnp.zeros((sizes.micro, channels), F32)
    dec_keep = jnp.zeros((sizes.micro, channels), F32)
    for index in range(sizes.micro):
        here = row == index
        times = jnp.where(here, times_ref[index].astype(F32), times)
        enc_keep = jnp.where(here, keep_ref[index, own].astype(F32), enc_keep)
        dec_keep = jnp.where(here, keep_ref[index, sections + own].astype(F32), dec_keep)
    enc_keep_out[...] = enc_keep
    dec_keep_out[...] = dec_keep
    level = noise_level(times)
    clean_part, noise_part = jnp.sqrt(level), jnp.sqrt(1.0 - level)
    for first in range(0, sizes.micro, 2):
        place = slice(first * sizes.length, (first + 2) * sizes.length)
        noise = noise_ref[place].astype(F32)
        mixed = []
        for index in (first, first + 1):
            clean = pool_ref[ids_ref[index]].astype(F32)
            own_noise = noise[sizes.sample(index - first)]
            mixed.append(
                clean_part[index : index + 1] * clean + noise_part[index : index + 1] * own_noise
            )
        start_out[place] = jnp.concatenate(mixed, axis=0).astype(BF16)
    for copy in copies:
        copy.wait()


def passing(kernel, scratch_count):
    def run(*refs):
        cut = len(refs) - scratch_count - 1
        kernel(*refs[:cut], *refs[cut + 1 :])

    return run


VM = pl.BlockSpec(memory_space=pltpu.VMEM)
ANY = pl.BlockSpec(memory_space=pl.ANY)


def params():
    return pltpu.CompilerParams(vmem_limit_bytes=VMEM_LIMIT)


def in_vmem(value):
    return pltpu.with_memory_space_constraint(value, pltpu.VMEM)


def staged_call(kernel, near, distant, plain_outs, kept, far, state, passed, scratch, flops):
    state = list(state) if state is not None else [None] * (len(kept) + len(far))
    inputs = [in_vmem(value) for value in near] + list(distant)
    in_specs = [VM] * len(near) + [ANY] * len(distant)
    aliases = {}
    for place, value in enumerate(state):
        if value is None:
            continue
        aliases[len(inputs)] = len(plain_outs) + place
        close = place < len(kept)
        inputs.append(in_vmem(value) if close else value)
        in_specs.append(VM if close else ANY)
    out_specs = [VM] * (len(plain_outs) + len(kept)) + [ANY] * len(far)
    out_shape = [pltpu.VMEM(s, d) for s, d in list(plain_outs) + list(kept)]
    out_shape += [jax.ShapeDtypeStruct(s, d) for s, d in far]
    if passed is not None:
        value, close = passed
        kernel = passing(kernel, len(scratch))
        aliases[len(inputs)] = len(out_specs)
        inputs.append(in_vmem(value) if close else value)
        in_specs.append(VM if close else ANY)
        out_specs.append(VM if close else ANY)
        kind = pltpu.VMEM if close else jax.ShapeDtypeStruct
        out_shape.append(kind(value.shape, value.dtype))
    outs = pl.pallas_call(
        kernel,
        in_specs=in_specs,
        out_specs=out_specs,
        out_shape=out_shape,
        scratch_shapes=scratch,
        input_output_aliases=aliases,
        compiler_params=params(),
        cost_estimate=pl.CostEstimate(flops=flops // COST_SHARE, bytes_accessed=0, transcendentals=0),
    )(*inputs)
    return list(outs[: len(plain_outs)]), list(outs[len(plain_outs) :])


def body(
    clip_pool,
    sample_ids,
    timesteps,
    noise_draw,
    keep_lists,
    enc_weight,
    enc_gain,
    dec_weight,
    dec_gain,
):
    sections = lax.axis_size("section")
    parts = lax.axis_size("dp")
    sizes = Sizes(noise_draw, sections)
    channels, rows, steps, total_rows = sizes.channels, sizes.rows, sizes.steps, sizes.total
    scale = 1.0 / math.sqrt(sizes.micro * parts * sizes.length)
    last = sections - 1

    def send(value, source, by, alone=False):
        pairs = [
            (other, (other + by) % sections)
            for other in range(source % PAIRS_APART, sections, PAIRS_APART)
        ]
        if alone:
            pairs = [(source, (source + by) % sections)]
        return lax.ppermute(value, "section", pairs)

    def mirrored(value):
        return lax.ppermute(value, "section", [(i, last - i) for i in range(sections)])

    def swapped(value, apart):
        return lax.ppermute(value, "dp", [(i, i ^ apart) for i in range(parts)])

    moves = []
    distances = [0]
    apart = parts // 2
    while apart:
        moves += [(place, apart) for place in range(len(distances))]
        distances += [distance ^ apart for distance in distances]
        apart //= 2

    clips = clip_pool.reshape(clip_pool.shape[0], sizes.length, channels)
    noise = noise_draw.reshape(total_rows, channels)
    enc_taps = enc_weight.reshape(3, 3 * channels, channels)
    dec_taps = dec_weight.reshape(DEC_TAPS * channels, channels)
    enc_taps, dec_taps, spread_matrix, start, enc_keep, dec_keep = pl.pallas_call(
        functools.partial(prologue_kernel, sizes, sections),
        in_specs=[ANY] * 3 + [VM] * 2 + [pl.BlockSpec(memory_space=pltpu.HBM)] * 2,
        out_specs=[VM] * 6,
        out_shape=[
            pltpu.VMEM(enc_taps.shape, BF16),
            pltpu.VMEM(dec_taps.shape, BF16),
            pltpu.VMEM((channels, channels), BF16),
            pltpu.VMEM(noise.shape, BF16),
            pltpu.VMEM((sizes.micro, channels), F32),
            pltpu.VMEM((sizes.micro, channels), F32),
        ],
        scratch_shapes=[
            pltpu.SMEM(sample_ids.shape, jnp.int32),
            pltpu.SMEM(timesteps.shape, jnp.int32),
            pltpu.SMEM(keep_lists.shape, jnp.int32),
            pltpu.SemaphoreType.DMA((5,)),
        ],
        compiler_params=params(),
    )(
        sample_ids,
        timesteps,
        keep_lists,
        clips,
        noise,
        pltpu.with_memory_space_constraint(enc_taps, pltpu.HBM),
        pltpu.with_memory_space_constraint(dec_taps, pltpu.HBM),
    )
    row_shape = ((rows, channels), BF16)
    all_rows = ((total_rows, channels), BF16)
    bulk_shape = ((3 * total_rows + 16, channels), BF16)
    norm_far = [((total_rows, channels), F32), ((sizes.micro, 1, channels), F32)]
    gain_kept = ((8, channels), F32)
    early_rows = (steps // 2) * rows
    early_shape = ((early_rows, channels), BF16)
    late_shape = ((total_rows - early_rows + 16, channels), BF16)
    work = [
        pltpu.VMEM((rows, channels), F32),
        pltpu.VMEM((rows, channels), F32),
        pltpu.VMEM((rows, channels), F32),
        pltpu.VMEM((sizes.per_step, 1, channels), F32),
        pltpu.VMEM((rows, channels), BF16),
        pltpu.SemaphoreType.DMA((3,)),
    ]
    cols = [pltpu.VMEM((3, rows, 3 * channels), BF16)] + work
    enc_flops = 2 * rows * ENC_TAPS * channels * channels
    dec_flops = 2 * rows * DEC_TAPS * channels * channels
    enc_consts = [enc_taps, enc_gain, enc_keep, spread_matrix]
    dec_consts = [dec_taps, dec_gain, dec_keep, spread_matrix]
    held = {}

    def stage(kernel, near, distant, kept, far, passed, scratch, flops):
        names = [name for name, _ in kept + far]
        (y,), state = staged_call(
            kernel,
            near,
            distant,
            [row_shape],
            [shape for _, shape in kept],
            [shape for _, shape in far],
            [held.get(name) for name in names],
            passed,
            scratch,
            flops,
        )
        held.update(zip(names + ["passed"], state))
        return y

    def enc_forward(level, step, x, tied, passed):
        return stage(
            functools.partial(enc_forward_kernel, sizes, level, step, level == last),
            [x] + enc_consts,
            tied,
            [("out", all_rows)] if level < last else [],
            [("enc_xhat", norm_far[0]), ("enc_rstd", norm_far[1]), ("bulk", bulk_shape)],
            passed,
            cols,
            enc_flops,
        )

    def dec_forward(level, step, x, tied, passed):
        final = level == last
        return stage(
            functools.partial(
                dec_forward_kernel, sizes, level, step, level == 0, scale if final else None
            ),
            [x] + dec_consts + [x if level == 0 else held["came"]] + ([noise] if final else []),
            tied,
            [],
            [("dec_xhat", norm_far[0]), ("dec_rstd", norm_far[1]), ("bulk", bulk_shape)],
            passed,
            work,
            dec_flops,
        )

    def dec_backward(level, step, g, tied, passed):
        return stage(
            functools.partial(dec_backward_kernel, sizes, level, step, level == 0),
            [g] + dec_consts,
            [held["dec_xhat"], held["dec_rstd"]] + tied,
            [("dec_gain", gain_kept)] + ([("skip", all_rows)] if level > 0 else []),
            [("bulk", bulk_shape)],
            passed,
            work,
            dec_flops,
        )

    def enc_backward(level, step, t, tied, passed):
        final = level == last
        early = [("early", early_shape)] if sizes.split(level, step) else []
        return stage(
            functools.partial(enc_backward_kernel, sizes, level, step, final),
            [t] + enc_consts + ([] if final else [held["came back"]]),
            [held["enc_xhat"], held["enc_rstd"]] + tied,
            [("enc_gain", gain_kept)],
            early + [("late", late_shape)],
            passed,
            cols,
            enc_flops,
        )

    chain = [(enc_forward, level, level) for level in range(sections)]
    chain += [(dec_forward, level, level) for level in range(sections)]
    chain += [(dec_backward, level, level) for level in reversed(range(sections))]
    chain += [(enc_backward, level, level) for level in reversed(range(sections))]
    starts = [0]
    for before, after in zip(chain, chain[1:]):
        starts.append(starts[-1] + (1 if before[2] == after[2] else steps))
    order = sorted(
        (starts[place] + step, step, place) for place in range(len(chain)) for step in range(steps)
    )

    dec_out_rows = DEC_TAPS * channels // parts
    dec_span = tap_span(dec_out_rows, channels, DEC_TAPS, parts)
    width = channels // parts
    values = {(0, step): start for step in range(steps)}
    early_far = None
    for _, step, place in order:
        run, level, section = chain[place]
        tied, passed = [], None
        turning = (run is enc_forward and level == last - 1) or (run is dec_backward and level == 1)
        if turning and step == steps - 1 and step > 1:
            tied = [values[place + 1, 0], values[place + 1, 1]]
        if run is dec_forward and level == 0 and step == 0:
            tied = [held["came"]]
        if run is enc_backward and level == last and step == 0:
            tied = [held["came back"]]
        if run is enc_backward and level == 0 and step == steps - 1:
            passed = (held["bulk"], False)
        if run is enc_backward and level == 0 and step == steps - 1 and early_far is not None:
            tied = [early_far]
        y = run(level, step, values[place, step], tied, passed)
        if turning and step == steps - 1:
            if run is enc_forward:
                held["came"] = mirrored(held["out"])
            else:
                held["came back"] = mirrored(held["skip"])
        if run is enc_backward and level == 0 and step == steps - 1:
            bulks = [held["passed"]]
        if run is enc_backward and level == 0 and step == steps // 2 - 1:
            early_far = swapped(held["early"], moves[0][1])
        if place + 1 < len(chain):
            target = chain[place + 1][2]
            by = 1 if run in (enc_forward, dec_forward) else -1
            alone = run is dec_backward and level == 1
            values[place + 1, step] = y if target == section else send(y, section, by, alone)
    for source, apart in moves:
        bulks.append(swapped(bulks[source], apart))
    dec_weight_out, dec_gain_out = pl.pallas_call(
        functools.partial(dec_weight_kernel, sizes, dec_span, dec_out_rows, parts),
        in_specs=[VM] * parts,
        out_specs=[VM] * 2,
        out_shape=[
            jax.ShapeDtypeStruct((dec_out_rows, channels), F32),
            jax.ShapeDtypeStruct((1, width), F32),
        ],
        scratch_shapes=[pltpu.VMEM((dec_span * channels, channels), F32)],
        compiler_params=params(),
        cost_estimate=pl.CostEstimate(
            flops=2 * dec_span * channels * channels * parts * total_rows,
            bytes_accessed=0,
            transcendentals=0,
        ),
    )(*[in_vmem(value) for value in bulks])
    earlies = [held["early"], early_far]
    for source, apart in moves[1:]:
        earlies.append(swapped(earlies[source], apart))
    lates = [held["late"]] + [swapped(held["late"], distance) for distance in distances[1:]]
    enc_out_rows = ENC_TAPS * channels // parts
    enc_span = tap_span(enc_out_rows, channels, ENC_TAPS, parts)
    enc_weight_out, enc_gain_out = pl.pallas_call(
        functools.partial(enc_weight_kernel, sizes, enc_span, enc_out_rows, parts),
        in_specs=[VM] * (3 * parts),
        out_specs=[VM] * 2,
        out_shape=[
            jax.ShapeDtypeStruct((enc_out_rows, channels), F32),
            jax.ShapeDtypeStruct((1, width), F32),
        ],
        scratch_shapes=[pltpu.VMEM((enc_span * channels, channels), F32)],
        compiler_params=params(),
        cost_estimate=pl.CostEstimate(
            flops=2 * enc_span * channels * channels * parts * total_rows,
            bytes_accessed=0,
            transcendentals=0,
        ),
    )(*[in_vmem(value) for value in bulks + earlies + lates])
    return (enc_weight_out[None], enc_gain_out, dec_weight_out[None], dec_gain_out)


def solution(mesh):
    placed = (
        P("dp", None, None, None, None),
        P("dp"),
        P("dp"),
        P("dp", None, None, None, None),
        P("dp", None),
        P("section", None, None),
        P("section", None),
        P("section", None, None),
        P("section", None),
    )
    return jax.shard_map(
        body,
        mesh=mesh,
        in_specs=placed,
        out_specs=(
            P("section", "dp", None),
            P("section", "dp"),
            P("section", "dp", None),
            P("section", "dp"),
        ),
        check_vma=False,
    )
```
